32 devices in a mesh: rel: 4 (over z), ent: 8 (over y, x, core).
Axes of the slice: x: 2, y: 2, z: 4, core: 2. Of those that a mesh axis runs over, the one named last changes fastest.
Arguments:
- features: bfloat16 [4096, 512], P('ent'), may hold values from -6 to 6
- w_self: bfloat16 [512, 512], replicated, may hold values from -0.25 to 0.25
- basis_mats: bfloat16 [16384, 512], replicated, may hold values from -0.046875 to 0.046875
- basis_coeffs: float32 [1000, 32], replicated, may hold values from -5 to 5
- group_rels: int32 [1000], P('rel'), may hold values from 0 to 999, each once
- rel_local: int32 [16384], P(('rel', 'ent')), may hold values from 0 to 249
- edge_src: int32 [16384], P(('rel', 'ent')), may hold values from 0 to 4095, as said below
- edge_dst: int32 [16384], P(('rel', 'ent')), may hold values from 0 to 4095, as said below
- block_counts: int32 [4, 8, 8], P('rel', 'ent'), may hold values from 1 to 64, as said below
- cotangent: bfloat16 [4096, 512], P('ent'), may hold values from -6 to 6
Outputs:
- activations: bfloat16 [4096, 512], P('ent')
- grad_features: bfloat16 [4096, 512], P('ent')
- grad_basis: float32 [16384, 512], P(('rel', 'ent'))
The draws below stay inside these ranges and needn't reach their ends.
Inputs may be any that keep to these rules, and one draw needn't show every extreme that they name: `edge_src`: slot i's source is owned by ent index (i // 512) % 8: it lies in [that index * 512, that index * 512 + 512). `edge_dst`: slot i's destination is owned by block index k = (i % 512) // 64: it lies in [k * 512, k * 512 + 512); within each aligned block of 64 slots the destinations are non-decreasing; the live slots of a block are its first block_counts ones. `block_counts`: one relation group, drawn from the seed, has every block full.
All inputs are finite; a program needn't handle non-finite values.
Results may differ from the reference program's by a relative error of at most 0.0059.
Values may be sent and summed in bfloat16 or wider, within the bound.
No kernel may reach another device: no remote copies, remote signals or barrier semaphores. Data moves between devices by JAX's collectives and lax.ppermute only.
A program may use at most 192 MiB of HBM per device.

```python
import jax
import jax.numpy as jnp
from jax import lax

D = 512
B = 32
RELS = 1000
ENT_DEV = 512
SLOT_DEV = 512
ENTS = 4096
CAP = 64
RPG = 250
EDGE_SLOTS = 16384
N_REL = 4
N_ENT = 8


def draw_edge_src(key, part):
    total_slots = SLOT_DEV * N_REL * N_ENT
    positions = jnp.arange(total_slots, dtype=jnp.int32)
    owner = positions // SLOT_DEV % N_ENT
    offsets = jax.random.randint(jax.random.fold_in(key, 11), (total_slots,), 0, ENT_DEV)
    return (owner * ENT_DEV + offsets).astype(jnp.int32)


def draw_edge_dst(key, part):
    block_cap = SLOT_DEV // N_ENT
    offsets = jax.random.randint(jax.random.fold_in(key, 13), (N_REL * N_ENT, N_ENT, block_cap), 0, ENT_DEV)
    offsets = jnp.sort(offsets, axis=-1)
    owner = jnp.arange(N_ENT, dtype=jnp.int32)[None, :, None]
    return (owner * ENT_DEV + offsets).reshape(-1).astype(jnp.int32)


def draw_block_counts(key, part):
    block_cap = SLOT_DEV // N_ENT
    heavy = jax.random.randint(jax.random.fold_in(key, 7), (), 0, N_REL)
    others = jax.random.randint(jax.random.fold_in(key, 8), (N_REL, N_ENT, N_ENT), 1, block_cap + 1)
    groups = jnp.arange(N_REL, dtype=jnp.int32)[:, None, None]
    return jnp.where(groups == heavy, block_cap, others).astype(jnp.int32)


def with_ends(result, stream_key, low, high):
    place = [jax.random.randint(jax.random.fold_in(stream_key, axis), (), 0, length) for axis, length in enumerate(result.shape)]
    widest = result.shape.index(max(result.shape))
    neighbour = place[:widest] + [(place[widest] + 1) % result.shape[widest]] + place[widest + 1:]
    return result.at[tuple(place)].set(low).at[tuple(neighbour)].set(high)


def level_of(own_key, extent, shards, least, largest):
    def one(position, shards_of):
        steps = jax.random.uniform(jax.random.fold_in(jax.random.fold_in(own_key, 6), position), (shards_of,), jnp.float32, least / len(shards), largest / len(shards))
        return jnp.repeat(jnp.exp(steps), extent[position] // shards_of).reshape((-1,) + (1,) * (len(extent) - position - 1))

    gain = one(*shards[0])
    for cut in shards[1:]:
        gain = gain * one(*cut)
    return gain


def noise(key, extent, width, bound, pieces=(), held_as=jnp.bfloat16):
    entries = jax.random.normal(key, extent, jnp.float32) * width
    if len(pieces) > 0:
        entries = level_of(key, extent, pieces, -0.22, 0.18) * entries
    return jnp.clip(entries, min=-bound, max=bound).astype(held_as)


def setup_inputs(seed: int = 0) -> dict:
    key_list = jax.random.split(jax.random.key(seed), 11)
    features = noise(key_list[0], (ENTS, D), 1.0, 6.0, ((0, 8),))
    w_self = noise(key_list[1], (D, D), D ** -0.5, 0.25)
    basis_mats = noise(key_list[2], (B * D, D), (B * D) ** -0.5, 0.046875)
    basis_coeffs = noise(key_list[3], (RELS, B), 1.0, 5.0, (), jnp.float32)
    group_rels = jax.random.permutation(key_list[4], RELS).astype(jnp.int32)
    rel_local = with_ends(jax.random.randint(key_list[5], (EDGE_SLOTS,), 0, RPG), jax.random.fold_in(key_list[5], 1), 0, RPG - 1).astype(jnp.int32)
    edge_src = draw_edge_src(jax.random.fold_in(key_list[10], 71), 0)
    edge_dst = draw_edge_dst(jax.random.fold_in(key_list[10], 71), 0)
    block_counts = draw_block_counts(jax.random.fold_in(key_list[10], 71), 0)
    cotangent = noise(key_list[9], (ENTS, D), 1.0, 6.0, ((0, 8),))
    return dict(features=features, w_self=w_self, basis_mats=basis_mats, basis_coeffs=basis_coeffs, group_rels=group_rels, rel_local=rel_local, edge_src=edge_src, edge_dst=edge_dst, block_counts=block_counts, cotangent=cotangent)


def reference(features, w_self, basis_mats, basis_coeffs, group_rels, rel_local, edge_src, edge_dst, block_counts, cotangent):
    ent_total = features.shape[0]
    block_total = N_REL * N_ENT
    slot_pos = jnp.arange(SLOT_DEV, dtype=jnp.int32) % CAP

    def block_data(index):
        group = index // N_ENT
        sender = index % N_ENT
        row_start = index * SLOT_DEV
        local_rel = lax.dynamic_slice_in_dim(rel_local, row_start, SLOT_DEV)
        src_block = lax.dynamic_slice_in_dim(edge_src, row_start, SLOT_DEV)
        limits = jnp.repeat(block_counts[group, sender], CAP, total_repeat_length=SLOT_DEV)
        is_live = slot_pos < limits
        rel_coef = basis_coeffs[group_rels[group * RPG + local_rel]]
        src_rows = features[src_block].astype(jnp.float32)
        mixed = (rel_coef[:, :, None] * src_rows[:, None, :]).reshape(SLOT_DEV, B * D).astype(jnp.bfloat16)
        return mixed, rel_coef, is_live

    def forward_block(index):
        mixed, rel_coef, is_live = block_data(index)
        product = jnp.dot(mixed, basis_mats, preferred_element_type=jnp.float32)
        return (product * is_live.astype(jnp.float32)[:, None]).astype(jnp.bfloat16)

    block_ids = jnp.arange(block_total, dtype=jnp.int32)
    messages = lax.map(forward_block, block_ids).reshape(-1, D)
    all_pos = jnp.arange(EDGE_SLOTS, dtype=jnp.int32) % CAP
    live_all = all_pos < jnp.repeat(block_counts.reshape(-1), CAP, total_repeat_length=EDGE_SLOTS)
    targets = jnp.where(live_all, edge_dst, ent_total)
    sums = jax.ops.segment_sum(messages.astype(jnp.float32), targets, ent_total + 1)[:ent_total]
    in_degree = jax.ops.segment_sum(live_all.astype(jnp.float32), targets, ent_total + 1)[:ent_total]
    inverse = 1.0 / jnp.maximum(in_degree, 1.0)
    pre_act = jnp.dot(features, w_self, preferred_element_type=jnp.float32) + sums * inverse[:, None]
    sigmoid_pre = jax.nn.sigmoid(pre_act)
    activations = (pre_act * sigmoid_pre).astype(jnp.bfloat16)
    grad_pre = (cotangent.astype(jnp.float32) * (sigmoid_pre * (1.0 + pre_act * (1.0 - sigmoid_pre)))).astype(jnp.bfloat16)
    grad_scaled = (grad_pre.astype(jnp.float32) * inverse[:, None]).astype(jnp.bfloat16)
    grad_back = jnp.where(live_all[:, None], grad_scaled[edge_dst], jnp.zeros((), jnp.bfloat16))

    def backward_block(carry, index):
        mixed, rel_coef, is_live = block_data(index)
        grad_block = lax.dynamic_slice_in_dim(grad_back, index * SLOT_DEV, SLOT_DEV)
        grad_mixed = lax.dot_general(grad_block, basis_mats, (((1,), (1,)), ((), ())), preferred_element_type=jnp.float32)
        grad_rows = jnp.sum(grad_mixed.reshape(SLOT_DEV, B, D) * rel_coef[:, :, None], axis=1)
        carry = carry + lax.dot_general(mixed, grad_block, (((0,), (0,)), ((), ())), preferred_element_type=jnp.float32)
        return carry, grad_rows

    grad_basis, grad_rows = lax.scan(backward_block, jnp.zeros((B * D, D), jnp.float32), block_ids)
    grad_src = jax.ops.segment_sum(grad_rows.reshape(-1, D), edge_src, ent_total)
    self_part = lax.dot_general(grad_pre, w_self, (((1,), (1,)), ((), ())), preferred_element_type=jnp.float32)
    grad_features = (self_part + grad_src).astype(jnp.bfloat16)
    return activations, grad_features, grad_basis
```

```python
import functools

import jax
import jax.numpy as jnp
from jax import lax
from jax.experimental import pallas as pl
from jax.experimental.pallas import tpu as pltpu
from jax.sharding import PartitionSpec as P

BF = jnp.bfloat16
F32 = jnp.float32
VMEM = pl.BlockSpec(memory_space=pltpu.VMEM)
SMEM = pl.BlockSpec(memory_space=pltpu.SMEM)
VMEM_LIMIT = 56 * 1024 * 1024
Z_SPLIT = 2
TABLE = 256


def dot(a, b):
    return jnp.dot(a, b, preferred_element_type=F32)


def dot_nt(a, b):
    return lax.dot_general(a, b, (((1,), (1,)), ((), ())), preferred_element_type=F32)


def one_hot(row, count):
    places = lax.broadcasted_iota(jnp.int32, (count, row.shape[1]), 0)
    return jnp.where(places == row, 1.0, 0.0).astype(BF)


def split3(x):
    high = x.astype(BF)
    rest = x - high.astype(F32)
    middle = rest.astype(BF)
    return high, middle, (rest - middle.astype(F32)).astype(BF)


def call(kernel, outs, ins, *args, scratch=(), flops=0, **more):
    size = sum(a.size * a.dtype.itemsize for a in args) + sum(o.size * o.dtype.itemsize for o in outs)
    return pl.pallas_call(
        kernel,
        out_shape=tuple(outs),
        in_specs=ins,
        out_specs=tuple(VMEM for _ in outs),
        scratch_shapes=scratch,
        compiler_params=pltpu.CompilerParams(vmem_limit_bytes=VMEM_LIMIT),
        cost_estimate=pl.CostEstimate(flops=flops, bytes_accessed=size, transcendentals=0),
        **more,
    )(*args)


def transpose_kernel(h_ref, in_ref, out_ref):
    out_ref[0] = in_ref[0].T


def transposed_columns(basis, half, cols):
    count, depth, _ = basis.shape
    return pl.pallas_call(
        transpose_kernel,
        grid_spec=pltpu.PrefetchScalarGridSpec(
            num_scalar_prefetch=1,
            grid=(count,),
            in_specs=[pl.BlockSpec((1, depth, cols), lambda i, h: (i, 0, h[0]))],
            out_specs=pl.BlockSpec((1, cols, depth), lambda i, h: (i, 0, 0)),
        ),
        out_shape=jax.ShapeDtypeStruct((count, cols, depth), BF),
        cost_estimate=pl.CostEstimate(flops=0, bytes_accessed=4 * count * cols * depth, transcendentals=0),
    )(half, basis)


def prep_kernel(pos_ref, meta_ref, coeffs_ref, slots_ref, coef_in_ref, coef_out_ref, coef_b_ref,
                table_ref, pieces_ref, own_ref, *, n_rel, n_ent):
    ent, own_basis = pos_ref[0], pos_ref[1]
    basis_count = coeffs_ref.shape[0]
    cap = meta_ref.shape[2] // n_ent
    lanes = n_rel * cap
    n_high = n_rel * TABLE // 128

    coeff3 = jnp.concatenate(split3(coeffs_ref[...]), axis=0)
    for g in range(n_rel):
        picks = one_hot(meta_ref[g * n_ent, 3:4, :TABLE], coeffs_ref.shape[1])
        got = dot(coeff3, picks)
        rows = got[:basis_count] + got[basis_count:2 * basis_count] + got[2 * basis_count:]
        for part in range(TABLE // 128):
            table_ref[g * (TABLE // 128) + part] = rows[:, part * 128:(part + 1) * 128]
    for i, piece in enumerate(split3(table_ref[...].reshape(n_high * basis_count, 128))):
        pieces_ref[pl.ds(i * n_high * basis_count, n_high * basis_count), :] = piece
    own_row = table_ref[:, pl.ds(own_basis, 1), :].reshape(n_high, 128)
    pad = jnp.zeros((16 - n_high, 128), F32) if n_high < 16 else None
    own_rows = own_row if pad is None else jnp.concatenate([own_row, pad], axis=0)
    own_ref[...] = jnp.concatenate(split3(own_rows), axis=0)

    def regroup(s, carry):
        for g in range(n_rel):
            block = meta_ref[g * n_ent + s]
            for k in range(n_ent):
                slots_ref[s, k, :, g * cap:(g + 1) * cap] = block[:, k * cap:(k + 1) * cap]
        return carry

    lax.fori_loop(0, n_ent, regroup, 0)
    group = lax.broadcasted_iota(jnp.int32, (1, lanes), 1) // cap

    def low_high(s, k):
        index = group * TABLE + slots_ref[s, k, 0:1, :]
        return one_hot(index % 128, 128), index // 128

    def every(s, k):
        low, high = low_high(s, k)
        got = dot(pieces_ref[...], low)
        n = n_high * basis_count
        got = got[:n] + got[n:2 * n] + got[2 * n:]
        total = jnp.zeros((basis_count, lanes), F32)
        for i in range(n_high):
            total += jnp.where(high == i, got[i * basis_count:(i + 1) * basis_count], 0.0)
        return total

    def ends(m, carry):
        coef_in_ref[m] = every(ent ^ m, ent)
        coef_out_ref[m] = every(ent, ent ^ m)
        return carry

    lax.fori_loop(0, n_ent, ends, 0)
    n_own = own_rows.shape[0]

    def pairs(i, carry):
        s = i // n_ent
        k = i % n_ent
        low, high = low_high(s, k)
        got = dot(own_ref[...], low)
        got = got[:n_own] + got[n_own:2 * n_own] + got[2 * n_own:]
        mine = lax.broadcasted_iota(jnp.int32, got.shape, 0) == high
        coef_b_ref[s, k] = jnp.sum(jnp.where(mine, got, 0.0), axis=0, keepdims=True)
        return carry

    lax.fori_loop(0, n_ent * n_ent, pairs, 0)


def gather_chunks(refs, layout, out_ref):
    if layout is None:
        return refs[0]
    at = 0
    for m, parts in enumerate(layout):
        row = 0
        for rows in parts:
            out_ref[m, row:row + rows, :] = refs[at][...]
            row, at = row + rows, at + 1
    return out_ref


def chunk_scratch(layout, n_ent, depth, ents):
    return pltpu.VMEM((1, 8, 128) if layout is None else (n_ent, depth, ents), BF)


def weighted(weights_ref, coef_ref, m, columns, acc_ref, group):
    basis_count, cols, depth = weights_ref.shape
    acc_ref[...] = jnp.zeros_like(acc_ref)
    for first in range(0, basis_count, group):
        got = dot(weights_ref[first:first + group].reshape(group * cols, depth), columns)
        part = got[:cols] * coef_ref[m, first:first + 1, :]
        for i in range(1, group):
            part += got[i * cols:(i + 1) * cols] * coef_ref[m, first + i:first + i + 1, :]
        acc_ref[...] += part


def forward_kernel(*refs, layout, n_ent, half_axis):
    n_parts = sum(len(p) for p in layout) if layout else 1
    (pos_ref, slots_ref, coef_ref, weights_ref, wself_ref, cot_ref) = refs[:6]
    chunk_refs = refs[6:6 + n_parts]
    out_ref, grad_ref = refs[6 + n_parts:8 + n_parts]
    feat_ref, acc_ref, msg_ref, hot_ref = refs[8 + n_parts:]
    ent = pos_ref[0]
    cols = weights_ref.shape[1]
    lanes = slots_ref.shape[3]
    feat_ref = gather_chunks(chunk_refs, layout, feat_ref)
    ents = feat_ref.shape[2]
    msg_ref[:, cols:, :] = jnp.ones((n_ent, msg_ref.shape[1] - cols, lanes), BF)

    def sender(m, carry):
        s = ent ^ m
        picked = dot(feat_ref[m], one_hot(slots_ref[s, ent, 1:2, :], ents)).astype(BF)
        weighted(weights_ref, coef_ref, m, picked, acc_ref, 1024 // cols)
        msg_ref[m, :cols, :] = acc_ref[...].astype(BF)
        hot_ref[m] = one_hot(slots_ref[s, ent, 2:3, :], ents)
        return carry

    lax.fori_loop(0, n_ent, sender, 0)
    sums = dot_nt(msg_ref[0], hot_ref[0])
    for m in range(1, n_ent):
        sums += dot_nt(msg_ref[m], hot_ref[m])
    inverse = 1.0 / jnp.maximum(sums[cols:cols + 1, :], 1.0)
    pre = dot(wself_ref[...], feat_ref[0]) + sums[:cols] * inverse
    sig = jax.nn.sigmoid(pre)
    out_ref[...] = (pre * sig).T.astype(BF)
    grad_ref[...] = (cot_ref[...].astype(F32) * (sig * (1.0 + pre * (1.0 - sig)))).astype(BF)


def scatter_kernel(*refs, layout, n_ent, rows):
    n_parts = sum(len(p) for p in layout) if layout else 1
    pos_ref, slots_ref, coef_ref = refs[:3]
    chunk_refs = refs[3:3 + n_parts]
    mix_out_ref, degree_ref = refs[3 + n_parts:5 + n_parts]
    feat_ref, mix_ref, hot_ref = refs[5 + n_parts:]
    ent = pos_ref[0]
    lanes = slots_ref.shape[3]
    feat_ref = gather_chunks(chunk_refs, layout, feat_ref)
    ents = feat_ref.shape[2]
    mix_ref[:, rows:, :] = jnp.ones((n_ent, mix_ref.shape[1] - rows, lanes), BF)
    first = pl.multiple_of(pos_ref[2], 128)

    def receiver(n, carry):
        k = ent ^ n

        for m in range(n_ent):
            s = ent ^ m
            hot = one_hot(slots_ref[s, k, 1:2, :], ents)
            got = dot(feat_ref[m, pl.ds(first, rows), :], hot)
            mix_ref[m, :rows, :] = (got * coef_ref[s, k]).astype(BF)
            hot_ref[m] = one_hot(slots_ref[s, k, 2:3, :], ents)
        total = dot_nt(mix_ref[0], hot_ref[0])
        for m in range(1, n_ent):
            total += dot_nt(mix_ref[m], hot_ref[m])
        mix_out_ref[n] = total[:rows].astype(BF)
        degree_ref[n] = total[rows:rows + 8]
        return carry

    lax.fori_loop(0, n_ent, receiver, 0)


def backward_kernel(*refs, layout, n_ent, basis_shape):
    n_parts = sum(len(p) for p in layout) if layout else 1
    (pos_ref, slots_ref, coef_ref, weights_ref, wself_ref, degree_ref) = refs[:6]
    chunk_refs = refs[6:6 + n_parts]
    out_ref, scaled_out_ref = refs[6 + n_parts:8 + n_parts]
    grad_ref, acc_ref, row_ref, hot_ref = refs[8 + n_parts:]
    ent = pos_ref[0]
    cols = weights_ref.shape[1]
    grad_ref = gather_chunks(chunk_refs, layout, grad_ref)
    ents = grad_ref.shape[2]
    self_part = dot(wself_ref[...], grad_ref[0])

    def receiver(n, carry):
        k = ent ^ n
        inverse = 1.0 / jnp.maximum(degree_ref[n, 0:1, :], 1.0)
        scaled = (grad_ref[n].astype(F32) * inverse).astype(BF)
        scaled_out_ref[n] = scaled
        picked = dot(scaled, one_hot(slots_ref[ent, k, 2:3, :], ents)).astype(BF)
        weighted(weights_ref, coef_ref, n, picked, acc_ref, 1024 // cols)
        total = acc_ref[...]
        high = total.astype(BF)
        row_ref[n, :cols, :] = high
        row_ref[n, cols:, :] = (total - high.astype(F32)).astype(BF)
        hot_ref[n] = one_hot(slots_ref[ent, k, 1:2, :], ents)
        return carry

    lax.fori_loop(0, n_ent, receiver, 0)
    sums = dot_nt(row_ref[0], hot_ref[0])
    for n in range(1, n_ent):
        sums += dot_nt(row_ref[n], hot_ref[n])
    out_ref[...] = (self_part + sums[:cols] + sums[cols:]).T.astype(BF)


def basis_kernel(mix_ref, scaled_ref, out_ref):
    total = dot_nt(mix_ref[0], scaled_ref[0])
    for n in range(1, mix_ref.shape[0]):
        total += dot_nt(mix_ref[n], scaled_ref[n])
    out_ref[...] = total


def exchange(x, mask, axis):
    count = lax.axis_size(axis)
    return lax.ppermute(x, axis, [(i, i ^ mask) for i in range(count)])


def plane_chunks(x):
    n_ent = lax.axis_size("ent")
    rows = x.shape[0]
    if n_ent == 8:
        a, b = exchange(x, 2, "ent"), exchange(x, 4, "ent")
        c = exchange(x, 1, "ent")
        top = exchange(b[:rows // 2], 2, "ent")
        low = exchange(a[rows // 2:], 4, "ent")
        ca, cb = exchange(a, 1, "ent"), exchange(b, 1, "ent")
        c_top, c_low = exchange(top, 1, "ent"), exchange(low, 1, "ent")
        return [[x], [c], [a], [ca], [b], [cb], [top, low], [c_top, c_low]]
    whole = lax.all_gather(x, "ent", axis=0)
    order = lax.axis_index("ent") ^ jnp.arange(n_ent, dtype=jnp.int32)
    return whole[order]


def flat(chunks):
    if not isinstance(chunks, list):
        return [chunks], None
    return [p for parts in chunks for p in parts], [[p.shape[0] for p in parts] for parts in chunks]


def join(own, half, split, axis):
    pieces = [own] + [exchange(own, m, "rel") for m in range(1, split)]
    if split == 1:
        return own
    if split == 2:
        swap = half == 1
        return jnp.concatenate(
            [jnp.where(swap, pieces[1], pieces[0]), jnp.where(swap, pieces[0], pieces[1])], axis=axis
        )
    size = own.shape[axis]
    shape = list(own.shape)
    shape[axis] = size * split
    whole = jnp.zeros(shape, own.dtype)
    for m, piece in enumerate(pieces):
        whole = lax.dynamic_update_slice_in_dim(whole, piece, (half ^ m) * size, axis)
    return whole


def per_device(features, w_self, basis_mats, basis_coeffs, group_rels, rel_local, edge_src,
               edge_dst, block_counts, cotangent):
    ents, depth = features.shape
    n_ent, n_rel = lax.axis_size("ent"), lax.axis_size("rel")
    ent, rel = lax.axis_index("ent"), lax.axis_index("rel")
    slots = rel_local.shape[0]
    cap = slots // n_ent
    lanes = n_rel * cap
    n_rels, basis_count = basis_coeffs.shape
    rows = basis_count * depth // (n_ent * n_rel)
    split = Z_SPLIT if n_rel % Z_SPLIT == 0 else 1
    cols = depth // split
    half = rel % split
    place = rel * n_ent + ent

    index = jnp.arange(slots, dtype=jnp.int32)
    limits = jnp.repeat(block_counts.reshape(n_ent), cap, total_repeat_length=slots)
    target = jnp.where(index % cap < limits, edge_dst - index // cap * ents, -1)
    meta = jnp.stack([
        rel_local,
        edge_src - ent * ents,
        target,
        jnp.pad(group_rels, (0, slots - group_rels.shape[0]), constant_values=-1),
    ])
    meta = lax.all_to_all(
        jnp.broadcast_to(meta[None], (n_rel * n_ent, 4, slots)), ("rel", "ent"), 0, 0, tiled=True
    )
    feat, feat_layout = flat(plane_chunks(features.T))

    first_row = place * rows
    pos = jnp.stack([ent, first_row // depth, first_row % depth]).astype(jnp.int32)
    half_arr = half.reshape(1).astype(jnp.int32)
    basis = basis_mats.reshape(basis_count, depth, depth)
    columns = transposed_columns(basis, half_arr, cols)
    own_rows = lax.dynamic_slice_in_dim(basis, half * cols, cols, axis=1)
    wself_t = lax.dynamic_slice_in_dim(w_self, half * cols, cols, axis=1).T
    wself_rows = lax.dynamic_slice_in_dim(w_self, half * cols, cols, axis=0)
    cot_t = lax.dynamic_slice_in_dim(cotangent, half * cols, cols, axis=1).T
    padded = -(-n_rels // 128) * 128
    coeffs_t = jnp.pad(basis_coeffs, ((0, padded - n_rels), (0, 0))).T

    n_high = n_rel * TABLE // 128
    per_end = jax.ShapeDtypeStruct((n_ent, basis_count, lanes), F32)
    grouped, coef_in, coef_out, coef_b = call(
        functools.partial(prep_kernel, n_rel=n_rel, n_ent=n_ent),
        [
            jax.ShapeDtypeStruct((n_ent, n_ent, 4, lanes), jnp.int32),
            per_end,
            per_end,
            jax.ShapeDtypeStruct((n_ent, n_ent, 1, lanes), F32),
        ],
        [SMEM, VMEM, VMEM],
        pos, meta, coeffs_t,
        scratch=[
            pltpu.VMEM((n_high, basis_count, 128), F32),
            pltpu.VMEM((3 * n_high * basis_count, 128), BF),
            pltpu.VMEM((3 * max(16, n_high), 128), BF),
        ],
        flops=10**9,
    )

    out_cols, grad_cols = call(
        functools.partial(forward_kernel, layout=feat_layout, n_ent=n_ent, half_axis=None),
        [jax.ShapeDtypeStruct((ents, cols), BF), jax.ShapeDtypeStruct((cols, ents), BF)],
        [SMEM] + [VMEM] * (5 + len(feat)),
        pos, grouped, coef_in, columns, wself_t, cot_t, *feat,
        scratch=[
            chunk_scratch(feat_layout, n_ent, depth, ents),
            pltpu.VMEM((cols, lanes), F32),
            pltpu.VMEM((n_ent, cols + 16, lanes), BF),
            pltpu.VMEM((n_ent, ents, lanes), BF),
        ],
        flops=2 * n_ent * lanes * basis_count * depth * cols,
    )
    grad_pre = join(grad_cols, half, split, 0)
    grads, grad_layout = flat(plane_chunks(grad_pre))

    mixed, degree = call(
        functools.partial(scatter_kernel, layout=feat_layout, n_ent=n_ent, rows=rows),
        [jax.ShapeDtypeStruct((n_ent, rows, ents), BF), jax.ShapeDtypeStruct((n_ent, 8, ents), F32)],
        [SMEM] + [VMEM] * (2 + len(feat)),
        pos, grouped, coef_b, *feat,
        scratch=[
            chunk_scratch(feat_layout, n_ent, depth, ents),
            pltpu.VMEM((n_ent, rows + 16, lanes), BF),
            pltpu.VMEM((n_ent, ents, lanes), BF),
        ],
        flops=4 * n_ent * n_ent * lanes * rows * ents,
    )

    grad_out, scaled = call(
        functools.partial(backward_kernel, layout=grad_layout, n_ent=n_ent, basis_shape=None),
        [jax.ShapeDtypeStruct((ents, cols), BF), jax.ShapeDtypeStruct((n_ent, depth, ents), BF)],
        [SMEM] + [VMEM] * (5 + len(grads)),
        pos, grouped, coef_out, own_rows, wself_rows, degree, *grads,
        scratch=[
            chunk_scratch(grad_layout, n_ent, depth, ents),
            pltpu.VMEM((cols, lanes), F32),
            pltpu.VMEM((n_ent, 2 * cols, lanes), BF),
            pltpu.VMEM((n_ent, ents, lanes), BF),
        ],
        flops=2 * n_ent * lanes * basis_count * depth * cols,
    )
    grad_features = join(grad_out, half, split, 1)
    activations = join(out_cols, half, split, 1)
    (grad_basis,) = call(
        basis_kernel,
        [jax.ShapeDtypeStruct((rows, depth), F32)],
        [VMEM, VMEM],
        mixed, scaled,
        flops=2 * n_ent * rows * ents * depth,
    )
    return activations, grad_features, grad_basis


def solution(mesh):
    placed = (
        P("ent", None),
        P(),
        P(),
        P(),
        P("rel"),
        P(("rel", "ent")),
        P(("rel", "ent")),
        P(("rel", "ent")),
        P("rel", "ent", None),
        P("ent", None),
    )
    return jax.shard_map(
        per_device,
        mesh=mesh,
        in_specs=placed,
        out_specs=(P("ent", None), P("ent", None), P(("rel", "ent"), None)),
        check_vma=False,
    )
```

```python
import functools

import jax
import jax.numpy as jnp
from jax import lax
from jax.experimental import pallas as pl
from jax.experimental.pallas import tpu as pltpu
from jax.sharding import PartitionSpec as P

BF = jnp.bfloat16
F32 = jnp.float32
VMEM = pl.BlockSpec(memory_space=pltpu.VMEM)
SMEM = pl.BlockSpec(memory_space=pltpu.SMEM)
ANY = pl.BlockSpec(memory_space=pl.ANY)
VMEM_LIMIT = 56 * 1024 * 1024
SPLIT = 2
TILE = 256
GATHER, SCATTER = 32, 33


def dot(a, b):
    return jnp.dot(a, b, preferred_element_type=F32)


def dot_nt(a, b):
    return lax.dot_general(a, b, (((1,), (1,)), ((), ())), preferred_element_type=F32)


def dot_tn(a, b):
    return lax.dot_general(a, b, (((0,), (0,)), ((), ())), preferred_element_type=F32)


def one_hot(row, count):
    places = lax.broadcasted_iota(jnp.int32, (count, row.shape[1]), 0)
    return jnp.where(places == row, 1.0, 0.0).astype(BF)


def one_hot_rows(column, count):
    places = lax.broadcasted_iota(jnp.int32, (column.shape[0], count), 1)
    return jnp.where(places == column, 1.0, 0.0).astype(BF)


def split3(x):
    high = x.astype(BF)
    rest = x - high.astype(F32)
    middle = rest.astype(BF)
    return high, middle, (rest - middle.astype(F32)).astype(BF)


def shape(dims, kind):
    return jax.ShapeDtypeStruct(dims, kind)


def call(kernel, outs, out_specs, ins, *args, scratch=(), flops=0):
    size = sum(a.size * a.dtype.itemsize for a in args) + sum(o.size * o.dtype.itemsize for o in outs)
    return pl.pallas_call(
        kernel,
        out_shape=tuple(outs),
        in_specs=ins,
        out_specs=tuple(out_specs),
        scratch_shapes=scratch,
        compiler_params=pltpu.CompilerParams(vmem_limit_bytes=VMEM_LIMIT),
        cost_estimate=pl.CostEstimate(flops=flops, bytes_accessed=size, transcendentals=0),
    )(*args)


def pack_kernel(counts_ref, rel_ref, src_ref, dst_ref, group_ref, out_ref, *, ents, n_ent):
    slots = rel_ref.shape[1]
    cap = slots // n_ent
    ent = lax.axis_index("ent")
    lane = lax.broadcasted_iota(jnp.int32, (1, slots), 1)
    block = lane // cap
    limit = jnp.zeros((1, slots), jnp.int32)
    last = jnp.zeros((1, slots), jnp.int32)
    for k in range(n_ent):
        limit = jnp.where(block == k, counts_ref[0, 0, k], limit)
        last = jnp.where(lane == k, counts_ref[0, 0, k], last)
    live = lane - block * cap < limit
    group = group_ref[...]
    digits = jnp.concatenate([group // 128, group % 128, jnp.zeros((14, group.shape[1]), jnp.int32)], axis=0)
    got = dot(digits.astype(F32).astype(BF), one_hot(rel_ref[...], group.shape[1])).astype(jnp.int32)
    packed = jnp.concatenate([
        got[0:1] * 128 + got[1:2],
        src_ref[...] - ent * ents,
        jnp.where(live, dst_ref[...] - block * ents, -1),
        last,
    ], axis=0)

    def put(i, carry):
        out_ref[i] = packed
        return carry

    lax.fori_loop(0, out_ref.shape[0], put, 0)


def table_kernel(pos_ref, coeffs_ref, pieces_ref, own_ref):
    basis_count = coeffs_ref.shape[0]
    n_high = coeffs_ref.shape[1] // 128
    values = coeffs_ref[...]
    mine = coeffs_ref[pl.ds(pos_ref[0], 1), :]
    n = n_high * basis_count
    for h in range(n_high):
        for i, piece in enumerate(split3(values[:, h * 128:(h + 1) * 128])):
            pieces_ref[i * n + h * basis_count:i * n + (h + 1) * basis_count, :] = piece
    own = [mine[:, h * 128:(h + 1) * 128] for h in range(n_high)]
    own.append(jnp.zeros((own_ref.shape[0] // 3 - n_high, 128), F32))
    own_ref[...] = jnp.concatenate(split3(jnp.concatenate(own, axis=0)), axis=0)


def coefficients(pieces, rel_row, basis_count, n_high):
    high = rel_row // 128
    got = dot(pieces, one_hot(rel_row % 128, 128))
    n = n_high * basis_count
    got = got[:n] + got[n:2 * n] + got[2 * n:]
    total = jnp.zeros((basis_count, rel_row.shape[1]), F32)
    for i in range(n_high):
        total += jnp.where(high == i, got[i * basis_count:(i + 1) * basis_count], 0.0)
    return total


def slot_rows(coef, gather, scatter):
    basis_count, lanes = coef.shape
    wide = -(-lanes // 128) * 128
    rows = jnp.concatenate(
        [coef, gather.astype(F32), scatter.astype(F32), jnp.zeros((128 - basis_count - 2, lanes), F32)], axis=0
    )
    if wide != lanes:
        rows = jnp.concatenate([rows, jnp.zeros((128, wide - lanes), F32)], axis=1)
    return rows.T[:lanes]


def clear_rows(ref):
    lane = lax.broadcasted_iota(jnp.int32, ref.shape, 1)
    ref[...] = jnp.where((lane == GATHER) | (lane == SCATTER), -1.0, 0.0)


def put_blocks(ref, rows, at, cap, counts):
    for g, count in enumerate(counts):
        ref[pl.ds(pl.multiple_of(at, 8), cap), :] = rows[g * cap:(g + 1) * cap]
        at = at + (count + 7) // 8 * 8
    return at


def prep_in_kernel(counts_ref, meta_ref, pieces_ref, rows_ref, ends_ref, *, n_rel, n_ent, ents, count):
    ent = lax.axis_index("ent")
    slots = meta_ref.shape[2]
    cap = slots // n_ent
    n_high = pieces_ref.shape[0] // (3 * count)
    clear_rows(rows_ref)

    def sender(m, at):
        s = ent ^ m
        ends_ref[m] = at
        block = jnp.concatenate(
            [pltpu.roll(meta_ref[g * n_ent + s], slots - ent * cap, 1)[:, :cap] for g in range(n_rel)], axis=1
        )
        coef = coefficients(pieces_ref[...], block[0:1, :], count, n_high)
        rows = slot_rows(coef, block[1:2, :] + m * ents, block[2:3, :])
        return put_blocks(rows_ref, rows, at, cap, [counts_ref[g * n_ent + s, ent] for g in range(n_rel)])

    ends_ref[n_ent] = lax.fori_loop(0, n_ent, sender, jnp.int32(0), unroll=n_ent <= 8)


def prep_rest_kernel(counts_ref, meta_ref, pieces_ref, own_ref, slots_ref, coef_b_ref, rows_ref, ends_ref,
                     *, n_rel, n_ent, ents, count):
    ent = lax.axis_index("ent")
    cap = meta_ref.shape[2] // n_ent
    lanes = n_rel * cap
    n_high = pieces_ref.shape[0] // (3 * count)
    n_own = own_ref.shape[0] // 3
    clear_rows(rows_ref)

    def regroup(s, carry):
        for g in range(n_rel):
            block = meta_ref[g * n_ent + s]
            for k in range(n_ent):
                slots_ref[s, k, :, g * cap:(g + 1) * cap] = block[:, k * cap:(k + 1) * cap]
        return carry

    lax.fori_loop(0, n_ent, regroup, 0)

    def receiver(n, at):
        k = ent ^ n
        ends_ref[n] = at
        block = slots_ref[ent, k]
        coef = coefficients(pieces_ref[...], block[0:1, :], count, n_high)
        live = block[2:3, :] >= 0
        rows = slot_rows(coef, jnp.where(live, block[2:3, :] + n * ents, -1), jnp.where(live, block[1:2, :], -1))
        return put_blocks(rows_ref, rows, at, cap, [counts_ref[g * n_ent + ent, k] for g in range(n_rel)])

    ends_ref[n_ent] = lax.fori_loop(0, n_ent, receiver, jnp.int32(0), unroll=n_ent <= 8)

    def sender(s, carry):
        rel = jnp.concatenate([slots_ref[s, k, 0:1, :] for k in range(n_ent)], axis=1)
        got = dot(own_ref[...], one_hot(rel % 128, 128))
        got = got[:n_own] + got[n_own:2 * n_own] + got[2 * n_own:]
        mine = lax.broadcasted_iota(jnp.int32, got.shape, 0) == rel // 128
        picked = jnp.sum(jnp.where(mine, got, 0.0), axis=0, keepdims=True)
        for k in range(n_ent):
            coef_b_ref[s, k] = picked[:, k * lanes:(k + 1) * lanes]
        return carry

    lax.fori_loop(0, n_ent, sender, 0, unroll=n_ent <= 8)


def chunk_copies(refs, places, out_ref, sems):
    copies = []
    for i, (ref, place) in enumerate(zip(refs, places, strict=True)):
        if place is None:
            target = out_ref
        else:
            target = out_ref.at[place[0], pl.ds(place[1], ref.shape[0])]
        copies.append(pltpu.make_async_copy(ref, target, sems.at[i]))
    return copies


def gather_rows(rows_ref, ends_ref, pick, out_ref, lanes, ents, n_ent):
    last = pl.multiple_of((tiles_of(ends_ref[n_ent]) - 1) * TILE, TILE)
    out_ref[pl.ds(last, TILE), :] = jnp.zeros((TILE, out_ref.shape[1]), F32)

    def chunk(m, carry):
        at = pl.multiple_of(ends_ref[m], 8)
        column = rows_ref[pl.ds(at, lanes), GATHER:GATHER + 1].astype(jnp.int32)
        pick(m, one_hot_rows(column - m * ents, ents), pl.ds(at, lanes))
        return carry

    lax.fori_loop(0, n_ent, chunk, 0, unroll=n_ent <= 8)


def apply_bases(picked, weight, rows_ref, start, count):
    total = None
    for b in range(count):
        part = weight(b, picked) * rows_ref[pl.ds(start, TILE), b:b + 1]
        total = part if total is None else total + part
    return total


def tiles_of(end):
    return (end + TILE - 1) // TILE


def forward_kernel(*refs, places, n_ent, count):
    n_parts = len(places)
    ends_ref, rows_ref, basis_ref, wself_ref, cot_ref = refs[:5]
    chunk_refs = refs[5:5 + n_parts]
    out_ref, grad_ref, scaled_ref = refs[5 + n_parts:8 + n_parts]
    feat_ref, weights_ref, x_ref, sums_ref, sems, weight_sems = refs[8 + n_parts:]
    cols = weights_ref.shape[2]
    ents = feat_ref.shape[1]
    half = lax.axis_index("rel") % SPLIT
    loads = chunk_copies(chunk_refs, places, feat_ref, sems)
    for c in loads:
        c.start()
    weights = [
        pltpu.make_async_copy(
            basis_ref.at[b, :, pl.ds(pl.multiple_of(half * cols, cols), cols)], weights_ref.at[b], weight_sems.at[b]
        )
        for b in range(count)
    ]
    sums_ref[...] = jnp.zeros_like(sums_ref)
    for c in loads:
        c.wait()
    for c in weights:
        c.start()

    def pick(m, hot, place):
        x_ref[place, :] = dot(hot, feat_ref[m])

    gather_rows(rows_ref, ends_ref, pick, x_ref, x_ref.shape[0] // n_ent, ents, n_ent)
    for c in weights:
        c.wait()

    def tile(t, carry):
        start = pl.multiple_of(t * TILE, TILE)
        picked = x_ref[pl.ds(start, TILE), :].astype(BF)

        def weight(b, value):
            return dot(value, weights_ref[b])

        sent = apply_bases(picked, weight, rows_ref, start, count).astype(BF)
        hot = one_hot_rows(rows_ref[pl.ds(start, TILE), SCATTER:SCATTER + 1].astype(jnp.int32), ents)
        sums_ref[...] += dot_tn(hot, jnp.concatenate([sent, jnp.ones((TILE, 128), BF)], axis=1))
        return carry

    lax.fori_loop(0, tiles_of(ends_ref[n_ent]), tile, 0)
    inverse = 1.0 / jnp.maximum(sums_ref[:, cols:cols + 1], 1.0)
    pre = dot(feat_ref[0], wself_ref[...]) + sums_ref[:, :cols] * inverse
    sig = jax.nn.sigmoid(pre)
    out_ref[...] = (pre * sig).astype(BF)
    grad = (cot_ref[...].astype(F32) * (sig * (1.0 + pre * (1.0 - sig)))).astype(BF)
    grad_ref[...] = grad
    scaled_ref[...] = (grad.astype(F32) * inverse).astype(BF)


def mix_kernel(*refs, places, n_ent, rows, chunks):
    n_parts = len(places)
    pos_ref, slots_ref, coef_ref = refs[:3]
    chunk_refs = refs[3:3 + n_parts]
    mix_out_ref = refs[3 + n_parts]
    feat_ref, mix_ref, hot_ref, sems = refs[4 + n_parts:]
    ent = lax.axis_index("ent")
    ents = feat_ref.shape[1]
    lanes = slots_ref.shape[3]
    loads = chunk_copies(chunk_refs, places, feat_ref, sems)
    for c in loads:
        c.start()
    for c in loads:
        c.wait()
    first = pl.multiple_of(pos_ref[1], 128)

    def receiver(i, carry):
        k = ent ^ (chunks[0] + i)
        for m in range(n_ent):
            s = ent ^ m
            at = slice(m * lanes, (m + 1) * lanes)
            got = dot_tn(feat_ref[m, :, pl.ds(first, rows)], one_hot(slots_ref[s, k, 1:2, :], ents))
            mix_ref[:, at] = (got * coef_ref[s, k]).astype(BF)
            hot_ref[:, at] = one_hot(slots_ref[s, k, 2:3, :], ents)
        mix_out_ref[i] = dot_nt(mix_ref[...], hot_ref[...]).astype(BF)
        return carry

    lax.fori_loop(0, chunks[1] - chunks[0], receiver, 0)


def backward_kernel(*refs, places, n_ent, count):
    n_parts = len(places)
    ends_ref, rows_ref, basis_ref, wself_ref, pre_ref, other_ref = refs[:6]
    chunk_refs = refs[6:6 + 2 * n_parts]
    out_ref = refs[6 + 2 * n_parts]
    grad_ref, weights_ref, h_ref, sums_ref, sems, weight_sems = refs[7 + 2 * n_parts:]
    cols = weights_ref.shape[1]
    ents = grad_ref.shape[2]
    half = lax.axis_index("rel") % SPLIT
    own_at = pl.multiple_of(half * cols, cols)
    other_at = pl.multiple_of((1 - half) * cols, cols)
    loads = chunk_copies(chunk_refs[:n_parts], places, grad_ref.at[0], sems.at[0])
    loads += chunk_copies(chunk_refs[n_parts:], places, grad_ref.at[1], sems.at[1])
    for c in loads:
        c.start()
    weights = [
        pltpu.make_async_copy(basis_ref.at[b, pl.ds(own_at, cols)], weights_ref.at[b], weight_sems.at[b])
        for b in range(count)
    ]
    sums_ref[...] = jnp.zeros_like(sums_ref)
    for c in loads:
        c.wait()
    for c in weights:
        c.start()

    def pick(n, hot, place):
        h_ref[place, pl.ds(own_at, cols)] = dot(hot, grad_ref[0, n])
        h_ref[place, pl.ds(other_at, cols)] = dot(hot, grad_ref[1, n])

    gather_rows(rows_ref, ends_ref, pick, h_ref, h_ref.shape[0] // n_ent, ents, n_ent)
    for c in weights:
        c.wait()

    def tile(t, carry):
        start = pl.multiple_of(t * TILE, TILE)
        picked = h_ref[pl.ds(start, TILE), :].astype(BF)

        def weight(b, value):
            return dot_nt(value, weights_ref[b])

        total = apply_bases(picked, weight, rows_ref, start, count)
        high = total.astype(BF)
        low = (total - high.astype(F32)).astype(BF)
        hot = one_hot_rows(rows_ref[pl.ds(start, TILE), SCATTER:SCATTER + 1].astype(jnp.int32), ents)
        sums_ref[...] += dot_tn(hot, high) + dot_tn(hot, low)
        return carry

    lax.fori_loop(0, tiles_of(ends_ref[n_ent]), tile, 0)
    self_part = dot_nt(pre_ref[...], wself_ref[:, pl.ds(own_at, cols)])
    self_part += dot_nt(other_ref[...], wself_ref[:, pl.ds(other_at, cols)])
    out_ref[...] = (self_part + sums_ref[...]).astype(BF)


def basis_kernel(*refs, places, n_mix):
    n_parts = len(places)
    mix_refs = refs[:n_mix]
    chunk_refs = refs[n_mix:n_mix + 2 * n_parts]
    out_ref = refs[n_mix + 2 * n_parts]
    grad_ref, sems = refs[n_mix + 2 * n_parts + 1:]
    cols = grad_ref.shape[3]
    half = lax.axis_index("rel") % SPLIT
    loads = chunk_copies(chunk_refs[:n_parts], places, grad_ref.at[0], sems.at[0])
    loads += chunk_copies(chunk_refs[n_parts:], places, grad_ref.at[1], sems.at[1])
    for c in loads:
        c.start()
    for c in loads:
        c.wait()
    for side in range(SPLIT):
        total, n = None, 0
        for mix in mix_refs:
            for i in range(mix.shape[0]):
                part = dot(mix[i], grad_ref[side, n])
                total = part if total is None else total + part
                n += 1
        at = (half if side == 0 else 1 - half) * cols
        out_ref[:, pl.ds(pl.multiple_of(at, cols), cols)] = total


def exchange(x, mask, axis):
    count = lax.axis_size(axis)
    return lax.ppermute(x, axis, [(i, i ^ mask) for i in range(count)])


def stacked(x):
    n_ent = lax.axis_size("ent")
    whole = lax.all_gather(x, "ent", axis=0)
    return whole[lax.axis_index("ent") ^ jnp.arange(n_ent, dtype=jnp.int32)]


def feature_chunks(x, first, second):
    if lax.axis_size("ent") != 8:
        return [second(first([stacked(x)]))[0]], [None]
    rows = x.shape[0] // 2
    a, b = first([exchange(x, 2, "ent"), exchange(x, 4, "ent")])
    c = exchange(x, 1, "ent")
    top, low = second([exchange(b[:rows], 2, "ent"), exchange(a[rows:], 4, "ent")])
    parts = [x, c, a, exchange(a, 1, "ent"), b, exchange(b, 1, "ent")]
    parts += [top, low, exchange(top, 1, "ent"), exchange(low, 1, "ent")]
    return parts, [(m, 0) for m in range(6)] + [(6, 0), (6, rows), (7, 0), (7, rows)]


def half_chunks(own, other_of, first, second, third):
    if lax.axis_size("ent") != 8:
        (other,) = first([other_of()])
        other = third(second([other]))[0]
        return [stacked(own)], [stacked(other)], [None]
    a0, b0, c0 = exchange(own, 2, "ent"), exchange(own, 4, "ent"), exchange(own, 1, "ent")
    other, a0, b0 = first([other_of(), a0, b0])
    a1, b1, c1 = exchange(other, 2, "ent"), exchange(other, 4, "ent"), exchange(other, 1, "ent")
    d0 = exchange(b0, 2, "ent")
    ca0, cb0 = exchange(a0, 1, "ent"), exchange(b0, 1, "ent")
    a1, b1, d0 = second([a1, b1, d0])
    d1 = exchange(a1, 4, "ent")
    ca1, cb1, cd0 = exchange(a1, 1, "ent"), exchange(b1, 1, "ent"), exchange(d0, 1, "ent")
    (d1,) = third([d1])
    return (
        [own, c0, a0, ca0, b0, cb0, d0, cd0],
        [other, c1, a1, ca1, b1, cb1, d1, exchange(d1, 1, "ent")],
        [(m, 0) for m in range(8)],
    )


def join(own, other, half):
    swap = half == 1
    return jnp.concatenate([jnp.where(swap, other, own), jnp.where(swap, own, other)], axis=1)


def per_device(features, w_self, basis_mats, basis_coeffs, group_rels, rel_local, edge_src,
               edge_dst, block_counts, cotangent):
    ents, depth = features.shape
    n_ent, n_rel = lax.axis_size("ent"), lax.axis_size("rel")
    slots = rel_local.shape[0]
    cap = slots // n_ent
    lanes = n_rel * cap
    n_rels, count = basis_coeffs.shape
    n_dev = n_rel * n_ent
    rows = count * depth // n_dev
    cols = depth // SPLIT
    rel = lax.axis_index("rel")
    half = rel % SPLIT
    all_lanes = n_ent * lanes

    (meta,) = call(
        functools.partial(pack_kernel, ents=ents, n_ent=n_ent),
        [shape((n_dev, 4, slots), jnp.int32)], [VMEM], [SMEM] + [VMEM] * 4,
        block_counts, rel_local[None], edge_src[None], edge_dst[None],
        group_rels[None],
    )
    meta = lax.all_to_all(meta, ("rel", "ent"), 0, 0, tiled=True)
    counts = meta[:, 3, :n_ent]

    first_row = (rel * n_ent + lax.axis_index("ent")) * rows
    pos = jnp.stack([first_row // depth, first_row % depth]).astype(jnp.int32)
    basis = basis_mats.reshape(count, depth, depth)
    wself_cols = lax.dynamic_slice_in_dim(w_self, half * cols, cols, axis=1)
    wself_rows = lax.dynamic_slice_in_dim(w_self, half * cols, cols, axis=0)
    cot = lax.dynamic_slice_in_dim(cotangent, half * cols, cols, axis=1)
    padded = -(-n_rels // 128) * 128
    coeffs_t = jnp.pad(basis_coeffs, ((0, padded - n_rels), (0, 0))).T

    n_high = padded // 128
    n_own = -(-(n_high + 1) // 16) * 16
    pieces, own_pieces = call(
        table_kernel,
        [shape((3 * n_high * count, 128), BF), shape((3 * n_own, 128), BF)],
        [VMEM, VMEM], [SMEM, VMEM], pos, coeffs_t,
    )
    row_shape = shape((all_lanes, 128), F32)
    ends_shape = shape((n_ent + 1,), jnp.int32)
    inputs = [pieces, own_pieces, wself_cols, cot]

    def beside_first(arrived):
        tied = lax.optimization_barrier((*arrived, *inputs))
        inputs[:] = tied[len(arrived):]
        return tied[:len(arrived)]

    def beside_second(arrived):
        pieces = inputs[0]
        made = call(
            functools.partial(prep_in_kernel, n_rel=n_rel, n_ent=n_ent, ents=ents, count=count),
            [row_shape, ends_shape], [VMEM, SMEM], [SMEM, VMEM, VMEM],
            counts, meta, pieces,
            flops=10**9,
        )
        tied = lax.optimization_barrier((*arrived, *made))
        inputs.extend(tied[len(arrived):])
        return tied[:len(arrived)]

    feats, feat_places = feature_chunks(features, beside_first, beside_second)
    pieces, own_pieces, wself_cols, cot, rows_in, ends_in = inputs
    part_sems = pltpu.SemaphoreType.DMA((len(feats),))
    out_cols, pre_cols, scaled_cols = call(
        functools.partial(forward_kernel, places=feat_places, n_ent=n_ent, count=count),
        [shape((ents, cols), BF)] * 3, [VMEM] * 3,
        [SMEM, VMEM, ANY, VMEM, VMEM] + [ANY] * len(feats),
        ends_in, rows_in, basis, wself_cols, cot, *feats,
        scratch=[
            pltpu.VMEM((n_ent, ents, depth), BF),
            pltpu.VMEM((count, depth, cols), BF),
            pltpu.VMEM((all_lanes, depth), F32),
            pltpu.VMEM((ents, cols + 128), F32),
            part_sems,
            pltpu.SemaphoreType.DMA((count,)),
        ],
        flops=2 * all_lanes * count * depth * cols,
    )
    other_pre = []
    made = []

    def tie(arrived, *others):
        tied = lax.optimization_barrier((*arrived, *others))
        made.extend(tied[len(arrived):])
        return tied[:len(arrived)]

    def prep_rest(arrived):
        return tie(arrived, *call(
            functools.partial(prep_rest_kernel, n_rel=n_rel, n_ent=n_ent, ents=ents, count=count),
            [shape((n_ent, n_ent, 4, lanes), jnp.int32), shape((n_ent, n_ent, 1, lanes), F32), row_shape, ends_shape],
            [VMEM, VMEM, VMEM, SMEM], [SMEM, VMEM, VMEM, VMEM],
            counts, meta, pieces, own_pieces,
            flops=10**9,
        ))

    def mix(arrived, low, high):
        grouped, coef_b = made[:2]
        return tie(arrived, *call(
            functools.partial(mix_kernel, places=feat_places, n_ent=n_ent, rows=rows, chunks=(low, high)),
            [shape((high - low, rows, ents), BF)], [VMEM],
            [SMEM, VMEM, VMEM] + [ANY] * len(feats),
            pos, grouped, coef_b, *feats,
            scratch=[
                pltpu.VMEM((n_ent, ents, depth), BF),
                pltpu.VMEM((rows, all_lanes), BF),
                pltpu.VMEM((ents, all_lanes), BF),
                part_sems,
            ],
            flops=4 * (high - low) * n_ent * lanes * rows * ents,
        ))

    def mix_first(arrived):
        other_pre.append(exchange(pre_cols, 1, "rel"))
        return mix(arrived, 0, n_ent // 2)

    own_parts, other_parts, places = half_chunks(
        scaled_cols, lambda: exchange(scaled_cols, 1, "rel"), prep_rest, mix_first,
        lambda arrived: mix(arrived, n_ent // 2, n_ent),
    )
    rows_out, ends_out = made[2:4]
    mixes = made[4:]
    (other_pre,) = other_pre

    grad_scratch = pltpu.VMEM((SPLIT, n_ent, ents, cols), BF)
    grad_sems = pltpu.SemaphoreType.DMA((SPLIT, len(own_parts)))
    (grad_cols,) = call(
        functools.partial(backward_kernel, places=places, n_ent=n_ent, count=count),
        [shape((ents, cols), BF)], [VMEM],
        [SMEM, VMEM, ANY, VMEM, VMEM, VMEM] + [ANY] * (2 * len(own_parts)),
        ends_out, rows_out, basis, wself_rows, pre_cols, other_pre, *own_parts, *other_parts,
        scratch=[
            grad_scratch,
            pltpu.VMEM((count, cols, depth), BF),
            pltpu.VMEM((all_lanes, depth), F32),
            pltpu.VMEM((ents, cols), F32),
            grad_sems,
            pltpu.SemaphoreType.DMA((count,)),
        ],
        flops=2 * all_lanes * count * depth * cols,
    )
    grad_features = join(grad_cols, exchange(grad_cols, 1, "rel"), half)
    activations = join(out_cols, exchange(out_cols, 1, "rel"), half)
    (grad_basis,) = call(
        functools.partial(basis_kernel, places=places, n_mix=len(mixes)),
        [shape((rows, depth), F32)], [VMEM],
        [VMEM] * len(mixes) + [ANY] * (2 * len(own_parts)),
        *mixes, *own_parts, *other_parts,
        scratch=[grad_scratch, grad_sems],
        flops=2 * n_ent * rows * ents * depth,
    )
    return activations, grad_features, grad_basis


def solution(mesh):
    placed = (
        P("ent", None),
        P(),
        P(),
        P(),
        P("rel"),
        P(("rel", "ent")),
        P(("rel", "ent")),
        P(("rel", "ent")),
        P("rel", "ent", None),
        P("ent", None),
    )
    return jax.shard_map(
        per_device,
        mesh=mesh,
        in_specs=placed,
        out_specs=(P("ent", None), P("ent", None), P(("rel", "ent"), None)),
        check_vma=False,
    )
```

```python
import functools

import jax
import jax.numpy as jnp
from jax import lax
from jax.experimental import pallas as pl
from jax.experimental.pallas import tpu as pltpu
from jax.sharding import PartitionSpec as P

BF = jnp.bfloat16
F32 = jnp.float32
VMEM = pl.BlockSpec(memory_space=pltpu.VMEM)
SMEM = pl.BlockSpec(memory_space=pltpu.SMEM)
ANY = pl.BlockSpec(memory_space=pl.ANY)
VMEM_LIMIT = 56 * 1024 * 1024
SPLIT = 2
TILE = 512
GATHER, SCATTER = 32, 33


def dot(a, b):
    return jnp.dot(a, b, preferred_element_type=F32)


def dot_nt(a, b):
    return lax.dot_general(a, b, (((1,), (1,)), ((), ())), preferred_element_type=F32)


def dot_tn(a, b):
    return lax.dot_general(a, b, (((0,), (0,)), ((), ())), preferred_element_type=F32)


def one_hot(row, count):
    places = lax.broadcasted_iota(jnp.int32, (count, row.shape[1]), 0)
    return jnp.where(places == row, 1.0, 0.0).astype(BF)


def one_hot_rows(column, count):
    places = lax.broadcasted_iota(jnp.int32, (column.shape[0], count), 1)
    return jnp.where(places == column, 1.0, 0.0).astype(BF)


def split3(x):
    high = x.astype(BF)
    rest = x - high.astype(F32)
    middle = rest.astype(BF)
    return high, middle, (rest - middle.astype(F32)).astype(BF)


def shape(dims, kind):
    return jax.ShapeDtypeStruct(dims, kind)


def call(kernel, outs, out_specs, ins, *args, scratch=(), flops=0):
    size = sum(a.size * a.dtype.itemsize for a in args) + sum(o.size * o.dtype.itemsize for o in outs)
    return pl.pallas_call(
        kernel,
        out_shape=tuple(outs),
        in_specs=ins,
        out_specs=tuple(out_specs),
        scratch_shapes=scratch,
        compiler_params=pltpu.CompilerParams(vmem_limit_bytes=VMEM_LIMIT),
        cost_estimate=pl.CostEstimate(flops=flops, bytes_accessed=size, transcendentals=0),
    )(*args)


def pack_kernel(counts_ref, rel_ref, src_ref, dst_ref, group_ref, out_ref, *, ents, n_ent):
    slots = rel_ref.shape[1]
    cap = slots // n_ent
    ent = lax.axis_index("ent")
    lane = lax.broadcasted_iota(jnp.int32, (1, slots), 1)
    block = lane // cap
    limit = jnp.zeros((1, slots), jnp.int32)
    last = jnp.zeros((1, slots), jnp.int32)
    for k in range(n_ent):
        limit = jnp.where(block == k, counts_ref[0, 0, k], limit)
        last = jnp.where(lane == k, counts_ref[0, 0, k], last)
    live = lane - block * cap < limit
    group = group_ref[...]
    digits = jnp.concatenate([group // 128, group % 128, jnp.zeros((14, group.shape[1]), jnp.int32)], axis=0)
    got = dot(digits.astype(F32).astype(BF), one_hot(rel_ref[...], group.shape[1])).astype(jnp.int32)
    packed = jnp.concatenate([
        got[0:1] * 128 + got[1:2],
        src_ref[...] - ent * ents,
        jnp.where(live, dst_ref[...] - block * ents, -1),
        last,
    ], axis=0)

    def put(i, carry):
        out_ref[i] = packed
        return carry

    lax.fori_loop(0, out_ref.shape[0], put, 0)


def table_kernel(pos_ref, coeffs_ref, pieces_ref, own_ref):
    basis_count = coeffs_ref.shape[0]
    n_high = coeffs_ref.shape[1] // 128
    values = coeffs_ref[...]
    mine = coeffs_ref[pl.ds(pos_ref[0], 1), :]
    n = n_high * basis_count
    for h in range(n_high):
        for i, piece in enumerate(split3(values[:, h * 128:(h + 1) * 128])):
            pieces_ref[i * n + h * basis_count:i * n + (h + 1) * basis_count, :] = piece
    own = [mine[:, h * 128:(h + 1) * 128] for h in range(n_high)]
    own.append(jnp.zeros((own_ref.shape[0] // 3 - n_high, 128), F32))
    own_ref[...] = jnp.concatenate(split3(jnp.concatenate(own, axis=0)), axis=0)


def coefficients(pieces, rel_row, basis_count, n_high):
    high = rel_row // 128
    got = dot(pieces, one_hot(rel_row % 128, 128))
    n = n_high * basis_count
    got = got[:n] + got[n:2 * n] + got[2 * n:]
    total = jnp.zeros((basis_count, rel_row.shape[1]), F32)
    for i in range(n_high):
        total += jnp.where(high == i, got[i * basis_count:(i + 1) * basis_count], 0.0)
    return total


def slot_rows(coef, gather, scatter):
    basis_count, lanes = coef.shape
    wide = -(-lanes // 128) * 128
    rows = jnp.concatenate(
        [coef, gather.astype(F32), scatter.astype(F32), jnp.zeros((128 - basis_count - 2, lanes), F32)], axis=0
    )
    if wide != lanes:
        rows = jnp.concatenate([rows, jnp.zeros((128, wide - lanes), F32)], axis=1)
    return rows.T[:lanes]


def clear_rows(ref):
    lane = lax.broadcasted_iota(jnp.int32, ref.shape, 1)
    ref[...] = jnp.where((lane == GATHER) | (lane == SCATTER), -1.0, 0.0)


def put_blocks(ref, rows, at, cap, counts):
    for g, count in enumerate(counts):
        ref[pl.ds(pl.multiple_of(at, 8), cap), :] = rows[g * cap:(g + 1) * cap]
        at = at + (count + 7) // 8 * 8
    return at


def prep_in_kernel(counts_ref, meta_ref, pieces_ref, rows_ref, ends_ref, *, n_rel, n_ent, ents, count):
    ent = lax.axis_index("ent")
    slots = meta_ref.shape[2]
    cap = slots // n_ent
    n_high = pieces_ref.shape[0] // (3 * count)
    clear_rows(rows_ref)

    def sender(m, at):
        s = ent ^ m
        ends_ref[m] = at
        block = jnp.concatenate(
            [pltpu.roll(meta_ref[g * n_ent + s], slots - ent * cap, 1)[:, :cap] for g in range(n_rel)], axis=1
        )
        coef = coefficients(pieces_ref[...], block[0:1, :], count, n_high)
        rows = slot_rows(coef, block[1:2, :] + m * ents, block[2:3, :])
        return put_blocks(rows_ref, rows, at, cap, [counts_ref[g * n_ent + s, ent] for g in range(n_rel)])

    ends_ref[n_ent] = lax.fori_loop(0, n_ent, sender, jnp.int32(0), unroll=n_ent <= 8)


def prep_rest_kernel(counts_ref, meta_ref, pieces_ref, own_ref, slots_ref, coef_b_ref, rows_ref, ends_ref,
                     *, n_rel, n_ent, ents, count):
    ent = lax.axis_index("ent")
    cap = meta_ref.shape[2] // n_ent
    lanes = n_rel * cap
    n_high = pieces_ref.shape[0] // (3 * count)
    n_own = own_ref.shape[0] // 3
    clear_rows(rows_ref)

    def regroup(s, carry):
        for g in range(n_rel):
            block = meta_ref[g * n_ent + s]
            for k in range(n_ent):
                slots_ref[s, k, :, g * cap:(g + 1) * cap] = block[:, k * cap:(k + 1) * cap]
        return carry

    lax.fori_loop(0, n_ent, regroup, 0, unroll=n_ent <= 8)

    def receiver(n, at):
        k = ent ^ n
        ends_ref[n] = at
        block = slots_ref[ent, k]
        coef = coefficients(pieces_ref[...], block[0:1, :], count, n_high)
        live = block[2:3, :] >= 0
        rows = slot_rows(coef, jnp.where(live, block[2:3, :] + n * ents, -1), jnp.where(live, block[1:2, :], -1))
        return put_blocks(rows_ref, rows, at, cap, [counts_ref[g * n_ent + ent, k] for g in range(n_rel)])

    ends_ref[n_ent] = lax.fori_loop(0, n_ent, receiver, jnp.int32(0), unroll=n_ent <= 8)

    def sender(s, carry):
        rel = jnp.concatenate([slots_ref[s, k, 0:1, :] for k in range(n_ent)], axis=1)
        got = dot(own_ref[...], one_hot(rel % 128, 128))
        got = got[:n_own] + got[n_own:2 * n_own] + got[2 * n_own:]
        mine = lax.broadcasted_iota(jnp.int32, got.shape, 0) == rel // 128
        picked = jnp.sum(jnp.where(mine, got, 0.0), axis=0, keepdims=True)
        for k in range(n_ent):
            coef_b_ref[s, k] = picked[:, k * lanes:(k + 1) * lanes]
        return carry

    lax.fori_loop(0, n_ent, sender, 0, unroll=n_ent <= 8)


def chunk_copies(refs, places, out_ref, sems):
    copies = []
    for i, (ref, place) in enumerate(zip(refs, places, strict=True)):
        if place is None:
            target = out_ref
        else:
            target = out_ref.at[place[0], pl.ds(place[1], ref.shape[0])]
        copies.append(pltpu.make_async_copy(ref, target, sems.at[i]))
    return copies


def gather_rows(rows_ref, ends_ref, pick, out_ref, lanes, ents, n_ent):
    last = pl.multiple_of((tiles_of(ends_ref[n_ent]) - 1) * TILE, TILE)
    out_ref[pl.ds(last, TILE), :] = jnp.zeros((TILE, out_ref.shape[1]), F32)

    def chunk(m, carry):
        at = pl.multiple_of(ends_ref[m], 8)
        column = rows_ref[pl.ds(at, lanes), GATHER:GATHER + 1].astype(jnp.int32)
        pick(m, one_hot_rows(column - m * ents, ents), pl.ds(at, lanes))
        return carry

    lax.fori_loop(0, n_ent, chunk, 0, unroll=n_ent <= 8)


def apply_bases(picked, weight, rows_ref, start, count):
    total = None
    for b in range(count):
        part = weight(b, picked) * rows_ref[pl.ds(start, TILE), b:b + 1]
        total = part if total is None else total + part
    return total


WAIT_STEPS = (0, 4, 12)


def waited(weights, weight):
    def run(b, value):
        if b in WAIT_STEPS:
            later = [x for x in WAIT_STEPS if x > b] + [len(weights)]
            for c in weights[b:later[0]]:
                c.wait()
        return weight(b, value)

    return run


def tiles_of(end):
    return (end + TILE - 1) // TILE


def forward_kernel(*refs, places, n_ent, count):
    n_parts = len(places)
    ends_ref, rows_ref, basis_ref, wself_ref, cot_ref = refs[:5]
    chunk_refs = refs[5:5 + n_parts]
    out_ref, grad_ref, scaled_ref = refs[5 + n_parts:8 + n_parts]
    feat_ref, weights_ref, x_ref, sums_ref, sems, weight_sems = refs[8 + n_parts:]
    cols = weights_ref.shape[2]
    ents = feat_ref.shape[1]
    half = lax.axis_index("rel") % SPLIT
    loads = chunk_copies(chunk_refs, places, feat_ref, sems)
    for c in loads:
        c.start()
    weights = [
        pltpu.make_async_copy(
            basis_ref.at[b, :, pl.ds(pl.multiple_of(half * cols, cols), cols)], weights_ref.at[b], weight_sems.at[b]
        )
        for b in range(count)
    ]
    sums_ref[...] = jnp.zeros_like(sums_ref)
    for c in loads:
        c.wait()
    for c in weights:
        c.start()

    def pick(m, hot, place):
        x_ref[place, :] = dot(hot, feat_ref[m])

    gather_rows(rows_ref, ends_ref, pick, x_ref, x_ref.shape[0] // n_ent, ents, n_ent)

    def weight(b, value):
        return dot(value, weights_ref[b])

    def tile(t, carry, weight=weight):
        start = pl.multiple_of(t * TILE, TILE)
        picked = x_ref[pl.ds(start, TILE), :].astype(BF)
        sent = apply_bases(picked, weight, rows_ref, start, count).astype(BF)
        hot = one_hot_rows(rows_ref[pl.ds(start, TILE), SCATTER:SCATTER + 1].astype(jnp.int32), ents)
        sums_ref[...] += dot_tn(hot, jnp.concatenate([sent, jnp.ones((TILE, 128), BF)], axis=1))
        return carry

    tile(0, 0, waited(weights, weight))
    lax.fori_loop(1, tiles_of(ends_ref[n_ent]), tile, 0)
    inverse = 1.0 / jnp.maximum(sums_ref[:, cols:cols + 1], 1.0)
    pre = dot(feat_ref[0], wself_ref[...]) + sums_ref[:, :cols] * inverse
    sig = jax.nn.sigmoid(pre)
    out_ref[...] = (pre * sig).astype(BF)
    grad = (cot_ref[...].astype(F32) * (sig * (1.0 + pre * (1.0 - sig)))).astype(BF)
    grad_ref[...] = grad
    scaled_ref[...] = (grad.astype(F32) * inverse).astype(BF)


def mix_kernel(*refs, places, n_ent, rows, chunks):
    n_parts = len(places)
    pos_ref, slots_ref, coef_ref = refs[:3]
    chunk_refs = refs[3:3 + n_parts]
    mix_out_ref = refs[3 + n_parts]
    feat_ref, mix_ref, hot_ref, sems = refs[4 + n_parts:]
    ent = lax.axis_index("ent")
    ents = feat_ref.shape[1]
    lanes = slots_ref.shape[3]
    loads = chunk_copies(chunk_refs, places, feat_ref, sems)
    for c in loads:
        c.start()
    for c in loads:
        c.wait()
    first = pl.multiple_of(pos_ref[1], 128)

    def receiver(i, carry):
        k = ent ^ (chunks[0] + i)
        for m in range(n_ent):
            s = ent ^ m
            at = slice(m * lanes, (m + 1) * lanes)
            got = dot_tn(feat_ref[m, :, pl.ds(first, rows)], one_hot(slots_ref[s, k, 1:2, :], ents))
            mix_ref[:, at] = (got * coef_ref[s, k]).astype(BF)
            hot_ref[:, at] = one_hot(slots_ref[s, k, 2:3, :], ents)
        mix_out_ref[i] = dot_nt(mix_ref[...], hot_ref[...]).astype(BF)
        return carry

    lax.fori_loop(0, chunks[1] - chunks[0], receiver, 0)


def backward_kernel(*refs, places, n_ent, count):
    n_parts = len(places)
    ends_ref, rows_ref, basis_ref, wself_ref, pre_ref, other_ref = refs[:6]
    chunk_refs = refs[6:6 + 2 * n_parts]
    out_ref = refs[6 + 2 * n_parts]
    grad_ref, weights_ref, h_ref, sums_ref, sems, weight_sems = refs[7 + 2 * n_parts:]
    cols = weights_ref.shape[1]
    ents = grad_ref.shape[2]
    half = lax.axis_index("rel") % SPLIT
    own_at = pl.multiple_of(half * cols, cols)
    other_at = pl.multiple_of((1 - half) * cols, cols)
    loads = chunk_copies(chunk_refs[:n_parts], places, grad_ref.at[0], sems.at[0])
    loads += chunk_copies(chunk_refs[n_parts:], places, grad_ref.at[1], sems.at[1])
    for c in loads:
        c.start()
    weights = [
        pltpu.make_async_copy(basis_ref.at[b, pl.ds(own_at, cols)], weights_ref.at[b], weight_sems.at[b])
        for b in range(count)
    ]
    sums_ref[...] = jnp.zeros_like(sums_ref)
    for c in loads:
        c.wait()
    for c in weights:
        c.start()

    def pick(n, hot, place):
        h_ref[place, pl.ds(own_at, cols)] = dot(hot, grad_ref[0, n])
        h_ref[place, pl.ds(other_at, cols)] = dot(hot, grad_ref[1, n])

    gather_rows(rows_ref, ends_ref, pick, h_ref, h_ref.shape[0] // n_ent, ents, n_ent)

    def weight(b, value):
        return dot_nt(value, weights_ref[b])

    def tile(t, carry, weight=weight):
        start = pl.multiple_of(t * TILE, TILE)
        picked = h_ref[pl.ds(start, TILE), :].astype(BF)
        total = apply_bases(picked, weight, rows_ref, start, count)
        high = total.astype(BF)
        low = (total - high.astype(F32)).astype(BF)
        hot = one_hot_rows(rows_ref[pl.ds(start, TILE), SCATTER:SCATTER + 1].astype(jnp.int32), ents)
        sums_ref[...] += dot_tn(hot, high) + dot_tn(hot, low)
        return carry

    tile(0, 0, waited(weights, weight))
    lax.fori_loop(1, tiles_of(ends_ref[n_ent]), tile, 0)
    self_part = dot_nt(pre_ref[...], wself_ref[:, pl.ds(own_at, cols)])
    self_part += dot_nt(other_ref[...], wself_ref[:, pl.ds(other_at, cols)])
    out_ref[...] = (self_part + sums_ref[...]).astype(BF)


def basis_kernel(*refs, places, n_mix):
    n_parts = len(places)
    mix_refs = refs[:n_mix]
    chunk_refs = refs[n_mix:n_mix + 2 * n_parts]
    out_ref = refs[n_mix + 2 * n_parts]
    grad_ref, sems = refs[n_mix + 2 * n_parts + 1:]
    cols = grad_ref.shape[3]
    half = lax.axis_index("rel") % SPLIT
    loads = chunk_copies(chunk_refs[:n_parts], places, grad_ref.at[0], sems.at[0])
    loads += chunk_copies(chunk_refs[n_parts:], places, grad_ref.at[1], sems.at[1])
    for c in loads:
        c.start()
    for c in loads:
        c.wait()
    for side in range(SPLIT):
        total, n = None, 0
        for mix in mix_refs:
            for i in range(mix.shape[0]):
                part = dot(mix[i], grad_ref[side, n])
                total = part if total is None else total + part
                n += 1
        at = (half if side == 0 else 1 - half) * cols
        out_ref[:, pl.ds(pl.multiple_of(at, cols), cols)] = total


def exchange(x, mask, axis):
    count = lax.axis_size(axis)
    return lax.ppermute(x, axis, [(i, i ^ mask) for i in range(count)])


def stacked(x):
    n_ent = lax.axis_size("ent")
    whole = lax.all_gather(x, "ent", axis=0)
    return whole[lax.axis_index("ent") ^ jnp.arange(n_ent, dtype=jnp.int32)]


def feature_chunks(x, first, second):
    if lax.axis_size("ent") != 8:
        return [second(first([stacked(x)]))[0]], [None]
    rows = x.shape[0] // 2
    a, b = first([exchange(x, 2, "ent"), exchange(x, 4, "ent")])
    c = exchange(x, 1, "ent")
    top, low = second([exchange(b[:rows], 2, "ent"), exchange(a[rows:], 4, "ent")])
    parts = [x, c, a, exchange(a, 1, "ent"), b, exchange(b, 1, "ent")]
    parts += [top, low, exchange(top, 1, "ent"), exchange(low, 1, "ent")]
    return parts, [(m, 0) for m in range(6)] + [(6, 0), (6, rows), (7, 0), (7, rows)]


def half_chunks(own, other_of, first, second, third):
    if lax.axis_size("ent") != 8:
        (other,) = third(second(first([other_of()])))
        return [stacked(own)], [stacked(other)], [None]
    a0, b0, d0, c0 = [exchange(own, m, "ent") for m in (2, 4, 6, 1)]
    other, a0, b0 = first([other_of(), a0, b0])
    a1, b1, d1, c1 = [exchange(other, m, "ent") for m in (2, 4, 6, 1)]
    ca0, cb0 = exchange(a0, 1, "ent"), exchange(b0, 1, "ent")
    d0, a1, b1, d1 = second([d0, a1, b1, d1])
    cd0, ca1, cb1, cd1 = third([exchange(x, 1, "ent") for x in (d0, a1, b1, d1)])
    return [own, c0, a0, ca0, b0, cb0, d0, cd0], [other, c1, a1, ca1, b1, cb1, d1, cd1], [(m, 0) for m in range(8)]


def join(own, other, half):
    swap = half == 1
    return jnp.concatenate([jnp.where(swap, other, own), jnp.where(swap, own, other)], axis=1)


def per_device(features, w_self, basis_mats, basis_coeffs, group_rels, rel_local, edge_src,
               edge_dst, block_counts, cotangent):
    ents, depth = features.shape
    n_ent, n_rel = lax.axis_size("ent"), lax.axis_size("rel")
    slots = rel_local.shape[0]
    cap = slots // n_ent
    lanes = n_rel * cap
    n_rels, count = basis_coeffs.shape
    n_dev = n_rel * n_ent
    rows = count * depth // n_dev
    cols = depth // SPLIT
    rel = lax.axis_index("rel")
    half = rel % SPLIT
    all_lanes = n_ent * lanes

    (meta,) = call(
        functools.partial(pack_kernel, ents=ents, n_ent=n_ent),
        [shape((n_dev, 4, slots), jnp.int32)], [VMEM], [SMEM] + [VMEM] * 4,
        block_counts, rel_local[None], edge_src[None], edge_dst[None],
        group_rels[None],
    )
    meta = lax.all_to_all(meta, ("rel", "ent"), 0, 0, tiled=True)
    counts = meta[:, 3, :n_ent]

    first_row = (rel * n_ent + lax.axis_index("ent")) * rows
    pos = jnp.stack([first_row // depth, first_row % depth]).astype(jnp.int32)
    basis = basis_mats.reshape(count, depth, depth)
    wself_cols = lax.dynamic_slice_in_dim(w_self, half * cols, cols, axis=1)
    wself_rows = lax.dynamic_slice_in_dim(w_self, half * cols, cols, axis=0)
    cot = lax.dynamic_slice_in_dim(cotangent, half * cols, cols, axis=1)
    padded = -(-n_rels // 128) * 128
    coeffs_t = jnp.pad(basis_coeffs, ((0, padded - n_rels), (0, 0))).T

    n_high = padded // 128
    n_own = -(-(n_high + 1) // 16) * 16
    pieces, own_pieces = call(
        table_kernel,
        [shape((3 * n_high * count, 128), BF), shape((3 * n_own, 128), BF)],
        [VMEM, VMEM], [SMEM, VMEM], pos, coeffs_t,
    )
    row_shape = shape((all_lanes, 128), F32)
    ends_shape = shape((n_ent + 1,), jnp.int32)
    inputs = [pieces, own_pieces, wself_cols, cot, wself_rows]

    def beside_first(arrived):
        tied = lax.optimization_barrier((*arrived, *inputs))
        inputs[:] = tied[len(arrived):]
        return tied[:len(arrived)]

    def beside_second(arrived):
        pieces = inputs[0]
        made = call(
            functools.partial(prep_in_kernel, n_rel=n_rel, n_ent=n_ent, ents=ents, count=count),
            [row_shape, ends_shape], [VMEM, SMEM], [SMEM, VMEM, VMEM],
            counts, meta, pieces,
            flops=10**9,
        )
        tied = lax.optimization_barrier((*arrived, *made))
        inputs.extend(tied[len(arrived):])
        return tied[:len(arrived)]

    feats, feat_places = feature_chunks(features, beside_first, beside_second)
    pieces, own_pieces, wself_cols, cot, wself_rows, rows_in, ends_in = inputs
    part_sems = pltpu.SemaphoreType.DMA((len(feats),))
    out_cols, pre_cols, scaled_cols = call(
        functools.partial(forward_kernel, places=feat_places, n_ent=n_ent, count=count),
        [shape((ents, cols), BF)] * 3, [VMEM] * 3,
        [SMEM, VMEM, ANY, VMEM, VMEM] + [ANY] * len(feats),
        ends_in, rows_in, basis, wself_cols, cot, *feats,
        scratch=[
            pltpu.VMEM((n_ent, ents, depth), BF),
            pltpu.VMEM((count, depth, cols), BF),
            pltpu.VMEM((all_lanes, depth), F32),
            pltpu.VMEM((ents, cols + 128), F32),
            part_sems,
            pltpu.SemaphoreType.DMA((count,)),
        ],
        flops=2 * all_lanes * count * depth * cols,
    )
    other_pre = []
    made = []

    def tie(arrived, *others):
        tied = lax.optimization_barrier((*arrived, *others))
        made.extend(tied[len(arrived):])
        return tied[:len(arrived)]

    def prep_rest(arrived):
        return tie(arrived, *call(
            functools.partial(prep_rest_kernel, n_rel=n_rel, n_ent=n_ent, ents=ents, count=count),
            [shape((n_ent, n_ent, 4, lanes), jnp.int32), shape((n_ent, n_ent, 1, lanes), F32), row_shape, ends_shape],
            [VMEM, VMEM, VMEM, SMEM], [SMEM, VMEM, VMEM, VMEM],
            counts, meta, pieces, own_pieces,
            flops=10**9,
        ))

    def mix(arrived, low, high):
        grouped, coef_b = made[:2]
        return tie(arrived, *call(
            functools.partial(mix_kernel, places=feat_places, n_ent=n_ent, rows=rows, chunks=(low, high)),
            [shape((high - low, rows, ents), BF)], [VMEM],
            [SMEM, VMEM, VMEM] + [ANY] * len(feats),
            pos, grouped, coef_b, *feats,
            scratch=[
                pltpu.VMEM((n_ent, ents, depth), BF),
                pltpu.VMEM((rows, all_lanes), BF),
                pltpu.VMEM((ents, all_lanes), BF),
                part_sems,
            ],
            flops=4 * (high - low) * n_ent * lanes * rows * ents,
        ))

    def mix_first(arrived):
        other_pre.append(exchange(pre_cols, 1, "rel"))
        return mix(arrived, 0, n_ent // 2)

    own_parts, other_parts, places = half_chunks(
        scaled_cols, lambda: exchange(scaled_cols, 1, "rel"), prep_rest, mix_first,
        lambda arrived: mix(arrived, n_ent // 2, n_ent),
    )
    rows_out, ends_out = made[2:4]
    mixes = made[4:]
    (other_pre,) = other_pre

    grad_scratch = pltpu.VMEM((SPLIT, n_ent, ents, cols), BF)
    grad_sems = pltpu.SemaphoreType.DMA((SPLIT, len(own_parts)))
    (grad_cols,) = call(
        functools.partial(backward_kernel, places=places, n_ent=n_ent, count=count),
        [shape((ents, cols), BF)], [VMEM],
        [SMEM, VMEM, ANY, VMEM, VMEM, VMEM] + [ANY] * (2 * len(own_parts)),
        ends_out, rows_out, basis, wself_rows, pre_cols, other_pre, *own_parts, *other_parts,
        scratch=[
            grad_scratch,
            pltpu.VMEM((count, cols, depth), BF),
            pltpu.VMEM((all_lanes, depth), F32),
            pltpu.VMEM((ents, cols), F32),
            grad_sems,
            pltpu.SemaphoreType.DMA((count,)),
        ],
        flops=2 * all_lanes * count * depth * cols,
    )
    grad_features = join(grad_cols, exchange(grad_cols, 1, "rel"), half)
    activations = join(out_cols, exchange(out_cols, 1, "rel"), half)
    (grad_basis,) = call(
        functools.partial(basis_kernel, places=places, n_mix=len(mixes)),
        [shape((rows, depth), F32)], [VMEM],
        [VMEM] * len(mixes) + [ANY] * (2 * len(own_parts)),
        *mixes, *own_parts, *other_parts,
        scratch=[grad_scratch, grad_sems],
        flops=2 * n_ent * rows * ents * depth,
    )
    return activations, grad_features, grad_basis


def solution(mesh):
    placed = (
        P("ent", None),
        P(),
        P(),
        P(),
        P("rel"),
        P(("rel", "ent")),
        P(("rel", "ent")),
        P(("rel", "ent")),
        P("rel", "ent", None),
        P("ent", None),
    )
    return jax.shard_map(
        per_device,
        mesh=mesh,
        in_specs=placed,
        out_specs=(P("ent", None), P("ent", None), P(("rel", "ent"), None)),
        check_vma=False,
    )
```

```python
import functools

import jax
import jax.numpy as jnp
from jax import lax
from jax.experimental import pallas as pl
from jax.experimental.pallas import tpu as pltpu
from jax.sharding import PartitionSpec as P

BF = jnp.bfloat16
F32 = jnp.float32
VMEM = pl.BlockSpec(memory_space=pltpu.VMEM)
SMEM = pl.BlockSpec(memory_space=pltpu.SMEM)
ANY = pl.BlockSpec(memory_space=pl.ANY)
VMEM_LIMIT = 56 * 1024 * 1024
SPLIT = 2
WIDE = 512
GATHER, SCATTER = 32, 33


def dot(a, b):
    return jnp.dot(a, b, preferred_element_type=F32)


def dot_nt(a, b):
    return lax.dot_general(a, b, (((1,), (1,)), ((), ())), preferred_element_type=F32)


def dot_tn(a, b):
    return lax.dot_general(a, b, (((0,), (0,)), ((), ())), preferred_element_type=F32)


def one_hot(row, count):
    places = lax.broadcasted_iota(jnp.int32, (count, row.shape[1]), 0)
    return jnp.where(places == row, 1.0, 0.0).astype(BF)


def one_hot_rows(column, count):
    places = lax.broadcasted_iota(jnp.int32, (column.shape[0], count), 1)
    return jnp.where(places == column, 1.0, 0.0).astype(BF)


def split3(x):
    high = x.astype(BF)
    rest = x - high.astype(F32)
    middle = rest.astype(BF)
    return high, middle, (rest - middle.astype(F32)).astype(BF)


def shape(dims, kind):
    return jax.ShapeDtypeStruct(dims, kind)


def call(kernel, outs, out_specs, ins, *args, scratch=(), flops=0):
    size = sum(a.size * a.dtype.itemsize for a in args) + sum(o.size * o.dtype.itemsize for o in outs)
    return pl.pallas_call(
        kernel,
        out_shape=tuple(outs),
        in_specs=ins,
        out_specs=tuple(out_specs),
        scratch_shapes=scratch,
        compiler_params=pltpu.CompilerParams(vmem_limit_bytes=VMEM_LIMIT),
        cost_estimate=pl.CostEstimate(flops=flops, bytes_accessed=size, transcendentals=0),
    )(*args)


def pack_kernel(counts_ref, rel_ref, src_ref, dst_ref, group_ref, out_ref, *, ents, n_ent):
    slots = rel_ref.shape[1]
    cap = slots // n_ent
    ent = lax.axis_index("ent")
    lane = lax.broadcasted_iota(jnp.int32, (1, slots), 1)
    block = lane // cap
    limit = jnp.zeros((1, slots), jnp.int32)
    last = jnp.zeros((1, slots), jnp.int32)
    for k in range(n_ent):
        limit = jnp.where(block == k, counts_ref[0, 0, k], limit)
        last = jnp.where(lane == k, counts_ref[0, 0, k], last)
    live = lane - block * cap < limit
    group = group_ref[...]
    digits = jnp.concatenate([group // 128, group % 128, jnp.zeros((14, group.shape[1]), jnp.int32)], axis=0)
    got = dot(digits.astype(F32).astype(BF), one_hot(rel_ref[...], group.shape[1])).astype(jnp.int32)
    packed = jnp.concatenate([
        got[0:1] * 128 + got[1:2],
        src_ref[...] - ent * ents,
        jnp.where(live, dst_ref[...] - block * ents, -1),
        last,
    ], axis=0)

    def put(i, carry):
        out_ref[i] = packed
        return carry

    lax.fori_loop(0, out_ref.shape[0], put, 0)


def table_kernel(pos_ref, coeffs_ref, pieces_ref, own_ref):
    basis_count = coeffs_ref.shape[0]
    n_high = coeffs_ref.shape[1] // 128
    values = coeffs_ref[...]
    mine = coeffs_ref[pl.ds(pos_ref[0], 1), :]
    n = n_high * basis_count
    for h in range(n_high):
        for i, piece in enumerate(split3(values[:, h * 128:(h + 1) * 128])):
            pieces_ref[i * n + h * basis_count:i * n + (h + 1) * basis_count, :] = piece
    own = [mine[:, h * 128:(h + 1) * 128] for h in range(n_high)]
    own.append(jnp.zeros((own_ref.shape[0] // 3 - n_high, 128), F32))
    own_ref[...] = jnp.concatenate(split3(jnp.concatenate(own, axis=0)), axis=0)


def coefficients(pieces, rel_row, basis_count, n_high):
    high = rel_row // 128
    got = dot(pieces, one_hot(rel_row % 128, 128))
    n = n_high * basis_count
    got = got[:n] + got[n:2 * n] + got[2 * n:]
    total = jnp.zeros((basis_count, rel_row.shape[1]), F32)
    for i in range(n_high):
        total += jnp.where(high == i, got[i * basis_count:(i + 1) * basis_count], 0.0)
    return total


def slot_rows(coef, gather, scatter):
    basis_count, lanes = coef.shape
    wide = -(-lanes // 128) * 128
    rows = jnp.concatenate(
        [coef, gather.astype(F32), scatter.astype(F32), jnp.zeros((128 - basis_count - 2, lanes), F32)], axis=0
    )
    if wide != lanes:
        rows = jnp.concatenate([rows, jnp.zeros((128, wide - lanes), F32)], axis=1)
    return rows.T[:lanes]


def clear_rows(ref):
    lane = lax.broadcasted_iota(jnp.int32, ref.shape, 1)
    ref[...] = jnp.where((lane == GATHER) | (lane == SCATTER), -1.0, 0.0)


def put_blocks(ref, rows, at, cap, counts):
    for g, count in enumerate(counts):
        ref[pl.ds(pl.multiple_of(at, 8), cap), :] = rows[g * cap:(g + 1) * cap]
        at = at + (count + 7) // 8 * 8
    return at


def prep_in_kernel(counts_ref, meta_ref, pieces_ref, rows_ref, ends_ref, *, n_rel, n_ent, ents, count):
    ent = lax.axis_index("ent")
    slots = meta_ref.shape[2]
    cap = slots // n_ent
    n_high = pieces_ref.shape[0] // (3 * count)
    clear_rows(rows_ref)

    def sender(m, at):
        s = ent ^ m
        ends_ref[m] = at
        block = jnp.concatenate(
            [pltpu.roll(meta_ref[g * n_ent + s], slots - ent * cap, 1)[:, :cap] for g in range(n_rel)], axis=1
        )
        coef = coefficients(pieces_ref[...], block[0:1, :], count, n_high)
        rows = slot_rows(coef, block[1:2, :] + m * ents, block[2:3, :])
        return put_blocks(rows_ref, rows, at, cap, [counts_ref[g * n_ent + s, ent] for g in range(n_rel)])

    ends_ref[n_ent] = lax.fori_loop(0, n_ent, sender, jnp.int32(0), unroll=n_ent <= 8)


def prep_rest_kernel(counts_ref, meta_ref, pieces_ref, own_ref, slots_ref, coef_b_ref, rows_ref, ends_ref,
                     *, n_rel, n_ent, ents, count):
    ent = lax.axis_index("ent")
    cap = meta_ref.shape[2] // n_ent
    lanes = n_rel * cap
    n_high = pieces_ref.shape[0] // (3 * count)
    n_own = own_ref.shape[0] // 3
    clear_rows(rows_ref)

    def regroup(s, carry):
        for g in range(n_rel):
            block = meta_ref[g * n_ent + s]
            for k in range(n_ent):
                slots_ref[s, k, :, g * cap:(g + 1) * cap] = block[:, k * cap:(k + 1) * cap]
        return carry

    lax.fori_loop(0, n_ent, regroup, 0, unroll=n_ent <= 8)

    def receiver(n, at):
        k = ent ^ n
        ends_ref[n] = at
        block = slots_ref[ent, k]
        coef = coefficients(pieces_ref[...], block[0:1, :], count, n_high)
        live = block[2:3, :] >= 0
        rows = slot_rows(coef, jnp.where(live, block[2:3, :] + n * ents, -1), jnp.where(live, block[1:2, :], -1))
        return put_blocks(rows_ref, rows, at, cap, [counts_ref[g * n_ent + ent, k] for g in range(n_rel)])

    ends_ref[n_ent] = lax.fori_loop(0, n_ent, receiver, jnp.int32(0), unroll=n_ent <= 8)

    def sender(s, carry):
        rel = jnp.concatenate([slots_ref[s, k, 0:1, :] for k in range(n_ent)], axis=1)
        got = dot(own_ref[...], one_hot(rel % 128, 128))
        got = got[:n_own] + got[n_own:2 * n_own] + got[2 * n_own:]
        mine = lax.broadcasted_iota(jnp.int32, got.shape, 0) == rel // 128
        picked = jnp.sum(jnp.where(mine, got, 0.0), axis=0, keepdims=True)
        for k in range(n_ent):
            coef_b_ref[s, k] = picked[:, k * lanes:(k + 1) * lanes]
        return carry

    lax.fori_loop(0, n_ent, sender, 0, unroll=n_ent <= 8)


def chunk_copies(refs, places, out_ref, sems):
    copies = []
    for i, (ref, place) in enumerate(zip(refs, places, strict=True)):
        if place is None:
            target = out_ref
        else:
            target = out_ref.at[place[0], pl.ds(place[1], ref.shape[0])]
        copies.append(pltpu.make_async_copy(ref, target, sems.at[i]))
    return copies


def gather_rows(rows_ref, ends_ref, pick, out_ref, lanes, ents, n_ent):
    last = jnp.minimum(ends_ref[n_ent] // WIDE, out_ref.shape[0] // WIDE - 1)
    out_ref[pl.ds(pl.multiple_of(last * WIDE, WIDE), WIDE), :] = jnp.zeros((WIDE, out_ref.shape[1]), F32)

    def chunk(m, carry):
        at = pl.multiple_of(ends_ref[m], 8)
        column = rows_ref[pl.ds(at, lanes), GATHER:GATHER + 1].astype(jnp.int32)
        pick(m, one_hot_rows(column - m * ents, ents), pl.ds(at, lanes))
        return carry

    lax.fori_loop(0, n_ent, chunk, 0, unroll=n_ent <= 8)


def apply_bases(picked, weight, rows_ref, start, size, count):
    total = None
    for b in range(count):
        part = weight(b, picked) * rows_ref[pl.ds(start, size), b:b + 1]
        total = part if total is None else total + part
    return total


WAIT_STEPS = (0, 4, 12)


def waited(weights, weight):
    def run(b, value):
        if b in WAIT_STEPS:
            later = [x for x in WAIT_STEPS if x > b] + [len(weights)]
            for c in weights[b:later[0]]:
                c.wait()
        return weight(b, value)

    return run


def for_tiles(end, narrow, tile, first):
    first(0, WIDE)
    wide = jnp.maximum(end // WIDE, 1)
    lax.fori_loop(1, wide, lambda t, c: (tile(pl.multiple_of(t * WIDE, WIDE), WIDE), c)[1], 0)
    done = wide * WIDE
    rest = (jnp.maximum(end - done, 0) + narrow - 1) // narrow
    lax.fori_loop(0, rest, lambda t, c: (tile(pl.multiple_of(done + t * narrow, narrow), narrow), c)[1], 0)


def forward_kernel(*refs, places, n_ent, count):
    n_parts = len(places)
    ends_ref, rows_ref, basis_ref, wself_ref, cot_ref = refs[:5]
    chunk_refs = refs[5:5 + n_parts]
    out_ref, grad_ref, scaled_ref = refs[5 + n_parts:8 + n_parts]
    feat_ref, weights_ref, x_ref, sums_ref, sems, weight_sems = refs[8 + n_parts:]
    cols = weights_ref.shape[2]
    ents = feat_ref.shape[1]
    half = lax.axis_index("rel") % SPLIT
    loads = chunk_copies(chunk_refs, places, feat_ref, sems)
    for c in loads:
        c.start()
    weights = [
        pltpu.make_async_copy(
            basis_ref.at[b, :, pl.ds(pl.multiple_of(half * cols, cols), cols)], weights_ref.at[b], weight_sems.at[b]
        )
        for b in range(count)
    ]
    sums_ref[...] = jnp.zeros_like(sums_ref)
    for c in loads:
        c.wait()
    for c in weights:
        c.start()

    def pick(m, hot, place):
        x_ref[place, :] = dot(hot, feat_ref[m])

    gather_rows(rows_ref, ends_ref, pick, x_ref, x_ref.shape[0] // n_ent, ents, n_ent)

    def weight(b, value):
        return dot(value, weights_ref[b])

    def tile(start, size, weight=weight):
        picked = x_ref[pl.ds(start, size), :].astype(BF)
        sent = apply_bases(picked, weight, rows_ref, start, size, count).astype(BF)
        hot = one_hot_rows(rows_ref[pl.ds(start, size), SCATTER:SCATTER + 1].astype(jnp.int32), ents)
        sums_ref[...] += dot_tn(hot, jnp.concatenate([sent, jnp.ones((size, 128), BF)], axis=1))

    for_tiles(ends_ref[n_ent], 128, tile, lambda start, size: tile(start, size, waited(weights, weight)))
    inverse = 1.0 / jnp.maximum(sums_ref[:, cols:cols + 1], 1.0)
    pre = dot(feat_ref[0], wself_ref[...]) + sums_ref[:, :cols] * inverse
    sig = jax.nn.sigmoid(pre)
    out_ref[...] = (pre * sig).astype(BF)
    grad = (cot_ref[...].astype(F32) * (sig * (1.0 + pre * (1.0 - sig)))).astype(BF)
    grad_ref[...] = grad
    scaled_ref[...] = (grad.astype(F32) * inverse).astype(BF)


def mix_chunks(first_row, slots_ref, coef_ref, feat_ref, mix_ref, hot_ref, out_ref, chunks):
    ent = lax.axis_index("ent")
    n_ent, ents = feat_ref.shape[:2]
    lanes = slots_ref.shape[3]
    rows = out_ref.shape[1]

    def receiver(i, carry):
        k = ent ^ (chunks[0] + i)
        for m in range(n_ent):
            s = ent ^ m
            at = slice(m * lanes, (m + 1) * lanes)
            got = dot_tn(feat_ref[m, :, pl.ds(first_row, rows)], one_hot(slots_ref[s, k, 1:2, :], ents))
            mix_ref[:, at] = (got * coef_ref[s, k]).astype(BF)
            hot_ref[:, at] = one_hot(slots_ref[s, k, 2:3, :], ents)
        out_ref[i] = dot_nt(mix_ref[...], hot_ref[...]).astype(BF)
        return carry

    lax.fori_loop(0, chunks[1] - chunks[0], receiver, 0)


def mix_kernel(*refs, places, chunks):
    n_parts = len(places)
    pos_ref, slots_ref, coef_ref = refs[:3]
    chunk_refs = refs[3:3 + n_parts]
    mix_out_ref = refs[3 + n_parts]
    feat_ref, mix_ref, hot_ref, sems = refs[4 + n_parts:]
    loads = chunk_copies(chunk_refs, places, feat_ref, sems)
    for c in loads:
        c.start()
    for c in loads:
        c.wait()
    mix_chunks(pl.multiple_of(pos_ref[1], 128), slots_ref, coef_ref, feat_ref, mix_ref, hot_ref, mix_out_ref, chunks)


def backward_kernel(*refs, places, n_ent, count):
    n_parts = len(places)
    ends_ref, rows_ref, basis_ref, wself_ref, pre_ref, other_ref = refs[:6]
    chunk_refs = refs[6:6 + 2 * n_parts]
    out_ref = refs[6 + 2 * n_parts]
    grad_ref, weights_ref, h_ref, sums_ref, sems, weight_sems = refs[7 + 2 * n_parts:]
    cols = weights_ref.shape[1]
    ents = grad_ref.shape[2]
    half = lax.axis_index("rel") % SPLIT
    own_at = pl.multiple_of(half * cols, cols)
    other_at = pl.multiple_of((1 - half) * cols, cols)
    loads = chunk_copies(chunk_refs[:n_parts], places, grad_ref.at[0], sems.at[0])
    loads += chunk_copies(chunk_refs[n_parts:], places, grad_ref.at[1], sems.at[1])
    for c in loads:
        c.start()
    weights = [
        pltpu.make_async_copy(basis_ref.at[b, pl.ds(own_at, cols)], weights_ref.at[b], weight_sems.at[b])
        for b in range(count)
    ]
    sums_ref[...] = jnp.zeros_like(sums_ref)
    for c in loads:
        c.wait()
    for c in weights:
        c.start()

    def pick(n, hot, place):
        h_ref[place, pl.ds(own_at, cols)] = dot(hot, grad_ref[0, n])
        h_ref[place, pl.ds(other_at, cols)] = dot(hot, grad_ref[1, n])

    gather_rows(rows_ref, ends_ref, pick, h_ref, h_ref.shape[0] // n_ent, ents, n_ent)

    def weight(b, value):
        return dot_nt(value, weights_ref[b])

    def tile(start, size, weight=weight):
        picked = h_ref[pl.ds(start, size), :].astype(BF)
        total = apply_bases(picked, weight, rows_ref, start, size, count)
        high = total.astype(BF)
        low = (total - high.astype(F32)).astype(BF)
        hot = one_hot_rows(rows_ref[pl.ds(start, size), SCATTER:SCATTER + 1].astype(jnp.int32), ents)
        sums_ref[...] += dot_tn(hot, high) + dot_tn(hot, low)

    for_tiles(ends_ref[n_ent], 256, tile, lambda start, size: tile(start, size, waited(weights, weight)))
    self_part = dot_nt(pre_ref[...], wself_ref[:, pl.ds(own_at, cols)])
    self_part += dot_nt(other_ref[...], wself_ref[:, pl.ds(other_at, cols)])
    out_ref[...] = (self_part + sums_ref[...]).astype(BF)


def basis_kernel(*refs, feat_places, places, chunks):
    n_feats, n_parts = len(feat_places), len(places)
    pos_ref, slots_ref, coef_ref, done_ref = refs[:4]
    feat_refs = refs[4:4 + n_feats]
    chunk_refs = refs[4 + n_feats:4 + n_feats + 2 * n_parts]
    out_ref = refs[4 + n_feats + 2 * n_parts]
    (feat_ref, mix_ref, hot_ref, grad_ref, early_ref, rest_ref, feat_sems, sems, early_sem) = (
        refs[5 + n_feats + 2 * n_parts:]
    )
    cols = grad_ref.shape[3]
    half = lax.axis_index("rel") % SPLIT
    feat_loads = chunk_copies(feat_refs, feat_places, feat_ref, feat_sems)
    loads = chunk_copies(chunk_refs[:n_parts], places, grad_ref.at[0], sems.at[0])
    loads += chunk_copies(chunk_refs[n_parts:], places, grad_ref.at[1], sems.at[1])
    loads.append(pltpu.make_async_copy(done_ref, early_ref, early_sem))
    for c in feat_loads:
        c.start()
    for c in feat_loads:
        c.wait()
    for c in loads:
        c.start()
    mix_chunks(pl.multiple_of(pos_ref[1], 128), slots_ref, coef_ref, feat_ref, mix_ref, hot_ref, rest_ref, chunks)
    for c in loads:
        c.wait()
    for side in range(SPLIT):
        total, n = None, 0
        for mix in (early_ref, rest_ref):
            for i in range(mix.shape[0]):
                part = dot(mix[i], grad_ref[side, n])
                total = part if total is None else total + part
                n += 1
        at = (half if side == 0 else 1 - half) * cols
        out_ref[:, pl.ds(pl.multiple_of(at, cols), cols)] = total


def exchange(x, mask, axis):
    count = lax.axis_size(axis)
    return lax.ppermute(x, axis, [(i, i ^ mask) for i in range(count)])


def stacked(x):
    n_ent = lax.axis_size("ent")
    whole = lax.all_gather(x, "ent", axis=0)
    return whole[lax.axis_index("ent") ^ jnp.arange(n_ent, dtype=jnp.int32)]


def feature_chunks(x, first, second):
    if lax.axis_size("ent") != 8:
        return [second(first([stacked(x)]))[0]], [None]
    rows = x.shape[0] // 2
    a, b = first([exchange(x, 2, "ent"), exchange(x, 4, "ent")])
    c = exchange(x, 1, "ent")
    top, low = second([exchange(b[:rows], 2, "ent"), exchange(a[rows:], 4, "ent")])
    parts = [x, c, a, exchange(a, 1, "ent"), b, exchange(b, 1, "ent")]
    parts += [top, low, exchange(top, 1, "ent"), exchange(low, 1, "ent")]
    return parts, [(m, 0) for m in range(6)] + [(6, 0), (6, rows), (7, 0), (7, rows)]


def half_chunks(own, other_of, first, second):
    if lax.axis_size("ent") != 8:
        (other,) = second(first([other_of()]))
        return [stacked(own)], [stacked(other)], [None]
    a0, b0, d0, c0 = [exchange(own, m, "ent") for m in (2, 4, 6, 1)]
    other, a0, b0, c0 = first([other_of(), a0, b0, c0])
    a1, b1, d1 = [exchange(other, m, "ent") for m in (2, 4, 6)]
    other, a0, b0, d0, a1, b1, d1 = second([other, a0, b0, d0, a1, b1, d1])
    c1, ca0, cb0, cd0, ca1, cb1, cd1 = [exchange(x, 1, "ent") for x in (other, a0, b0, d0, a1, b1, d1)]
    return [own, c0, a0, ca0, b0, cb0, d0, cd0], [other, c1, a1, ca1, b1, cb1, d1, cd1], [(m, 0) for m in range(8)]


def join_kernel(*refs):
    n = len(refs) // 3
    half = lax.axis_index("rel") % SPLIT
    for own, other, out in zip(refs[:n], refs[n:2 * n], refs[2 * n:], strict=True):
        cols = own.shape[1]
        out[:, pl.ds(pl.multiple_of(half * cols, cols), cols)] = own[...]
        out[:, pl.ds(pl.multiple_of((1 - half) * cols, cols), cols)] = other[...]


def per_device(features, w_self, basis_mats, basis_coeffs, group_rels, rel_local, edge_src,
               edge_dst, block_counts, cotangent):
    ents, depth = features.shape
    n_ent, n_rel = lax.axis_size("ent"), lax.axis_size("rel")
    slots = rel_local.shape[0]
    cap = slots // n_ent
    lanes = n_rel * cap
    n_rels, count = basis_coeffs.shape
    n_dev = n_rel * n_ent
    rows = count * depth // n_dev
    cols = depth // SPLIT
    rel = lax.axis_index("rel")
    half = rel % SPLIT
    all_lanes = n_ent * lanes

    (meta,) = call(
        functools.partial(pack_kernel, ents=ents, n_ent=n_ent),
        [shape((n_dev, 4, slots), jnp.int32)], [VMEM], [SMEM] + [VMEM] * 4,
        block_counts, rel_local[None], edge_src[None], edge_dst[None],
        group_rels[None],
    )
    meta = lax.all_to_all(meta, ("rel", "ent"), 0, 0, tiled=True)
    counts = meta[:, 3, :n_ent]

    first_row = (rel * n_ent + lax.axis_index("ent")) * rows
    pos = jnp.stack([first_row // depth, first_row % depth]).astype(jnp.int32)
    basis = basis_mats.reshape(count, depth, depth)
    wself_cols = lax.dynamic_slice_in_dim(w_self, half * cols, cols, axis=1)
    wself_rows = lax.dynamic_slice_in_dim(w_self, half * cols, cols, axis=0)
    cot = lax.dynamic_slice_in_dim(cotangent, half * cols, cols, axis=1)
    padded = -(-n_rels // 128) * 128
    coeffs_t = jnp.pad(basis_coeffs, ((0, padded - n_rels), (0, 0))).T

    n_high = padded // 128
    n_own = -(-(n_high + 1) // 16) * 16
    pieces, own_pieces = call(
        table_kernel,
        [shape((3 * n_high * count, 128), BF), shape((3 * n_own, 128), BF)],
        [VMEM, VMEM], [SMEM, VMEM], pos, coeffs_t,
    )
    row_shape = shape((all_lanes, 128), F32)
    ends_shape = shape((n_ent + 1,), jnp.int32)
    inputs = [pieces, own_pieces, wself_cols, cot, wself_rows]

    def beside_first(arrived):
        tied = lax.optimization_barrier((*arrived, *inputs))
        inputs[:] = tied[len(arrived):]
        return tied[:len(arrived)]

    def beside_second(arrived):
        pieces = inputs[0]
        made = call(
            functools.partial(prep_in_kernel, n_rel=n_rel, n_ent=n_ent, ents=ents, count=count),
            [row_shape, ends_shape], [VMEM, SMEM], [SMEM, VMEM, VMEM],
            counts, meta, pieces,
            flops=10**9,
        )
        tied = lax.optimization_barrier((*arrived, *made))
        inputs.extend(tied[len(arrived):])
        return tied[:len(arrived)]

    feats, feat_places = feature_chunks(features, beside_first, beside_second)
    pieces, own_pieces, wself_cols, cot, wself_rows, rows_in, ends_in = inputs
    part_sems = pltpu.SemaphoreType.DMA((len(feats),))
    out_cols, pre_cols, scaled_cols = call(
        functools.partial(forward_kernel, places=feat_places, n_ent=n_ent, count=count),
        [shape((ents, cols), BF)] * 3, [VMEM] * 3,
        [SMEM, VMEM, ANY, VMEM, VMEM] + [ANY] * len(feats),
        ends_in, rows_in, basis, wself_cols, cot, *feats,
        scratch=[
            pltpu.VMEM((n_ent, ents, depth), BF),
            pltpu.VMEM((count, depth, cols), BF),
            pltpu.VMEM((all_lanes, depth), F32),
            pltpu.VMEM((ents, cols + 128), F32),
            part_sems,
            pltpu.SemaphoreType.DMA((count,)),
        ],
        flops=2 * all_lanes * count * depth * cols,
    )
    other_pre = []
    made = []

    def tie(arrived, *others):
        tied = lax.optimization_barrier((*arrived, *others))
        made.extend(tied[len(arrived):])
        return tied[:len(arrived)]

    def prep_rest(arrived):
        return tie(arrived, *call(
            functools.partial(prep_rest_kernel, n_rel=n_rel, n_ent=n_ent, ents=ents, count=count),
            [shape((n_ent, n_ent, 4, lanes), jnp.int32), shape((n_ent, n_ent, 1, lanes), F32), row_shape, ends_shape],
            [VMEM, VMEM, VMEM, SMEM], [SMEM, VMEM, VMEM, VMEM],
            counts, meta, pieces, own_pieces,
            flops=10**9,
        ))

    early = n_ent * 5 // 8
    mix_scratch = [
        pltpu.VMEM((n_ent, ents, depth), BF),
        pltpu.VMEM((rows, all_lanes), BF),
        pltpu.VMEM((ents, all_lanes), BF),
    ]

    def mix_early(arrived):
        other_pre.append(exchange(pre_cols, 1, "rel"))
        grouped, coef_b = made[:2]
        return tie(arrived, *call(
            functools.partial(mix_kernel, places=feat_places, chunks=(0, early)),
            [shape((early, rows, ents), BF)], [VMEM],
            [SMEM, VMEM, VMEM] + [ANY] * len(feats),
            pos, grouped, coef_b, *feats,
            scratch=mix_scratch + [part_sems],
            flops=10**9,
        ))

    own_parts, other_parts, places = half_chunks(
        scaled_cols, lambda: exchange(scaled_cols, 1, "rel"), prep_rest, mix_early
    )
    grouped, coef_b, rows_out, ends_out, mixed = made
    (other_pre,) = other_pre

    grad_scratch = pltpu.VMEM((SPLIT, n_ent, ents, cols), BF)
    grad_sems = pltpu.SemaphoreType.DMA((SPLIT, len(own_parts)))
    (grad_cols,) = call(
        functools.partial(backward_kernel, places=places, n_ent=n_ent, count=count),
        [shape((ents, cols), BF)], [VMEM],
        [SMEM, VMEM, ANY, VMEM, VMEM, VMEM] + [ANY] * (2 * len(own_parts)),
        ends_out, rows_out, basis, wself_rows, pre_cols, other_pre, *own_parts, *other_parts,
        scratch=[
            grad_scratch,
            pltpu.VMEM((count, cols, depth), BF),
            pltpu.VMEM((all_lanes, depth), F32),
            pltpu.VMEM((ents, cols), F32),
            grad_sems,
            pltpu.SemaphoreType.DMA((count,)),
        ],
        flops=2 * all_lanes * count * depth * cols,
    )
    grad_cols, out_cols, pos = lax.optimization_barrier((grad_cols, out_cols, pos))
    other_grad, other_out = exchange(grad_cols, 1, "rel"), exchange(out_cols, 1, "rel")
    (grad_basis,) = call(
        functools.partial(basis_kernel, feat_places=feat_places, places=places, chunks=(early, n_ent)),
        [shape((rows, depth), F32)], [VMEM],
        [SMEM, VMEM, VMEM] + [ANY] * (1 + len(feats) + 2 * len(own_parts)),
        pos, grouped, coef_b, mixed, *feats, *own_parts, *other_parts,
        scratch=mix_scratch + [
            grad_scratch,
            pltpu.VMEM((early, rows, ents), BF),
            pltpu.VMEM((n_ent - early, rows, ents), BF),
            part_sems,
            grad_sems,
            pltpu.SemaphoreType.DMA,
        ],
        flops=2 * n_ent * rows * ents * depth,
    )
    activations, grad_features = call(
        join_kernel, [shape((ents, depth), BF)] * 2, [VMEM] * 2, [VMEM] * 4, out_cols, grad_cols, other_out, other_grad
    )
    return activations, grad_features, grad_basis


def solution(mesh):
    placed = (
        P("ent", None),
        P(),
        P(),
        P(),
        P("rel"),
        P(("rel", "ent")),
        P(("rel", "ent")),
        P(("rel", "ent")),
        P("rel", "ent", None),
        P("ent", None),
    )
    return jax.shard_map(
        per_device,
        mesh=mesh,
        in_specs=placed,
        out_specs=(P("ent", None), P("ent", None), P(("rel", "ent"), None)),
        check_vma=False,
    )
```

```python
import functools

import jax
import jax.numpy as jnp
from jax import lax
from jax.experimental import pallas as pl
from jax.experimental.pallas import tpu as pltpu
from jax.sharding import PartitionSpec as P

BF = jnp.bfloat16
F32 = jnp.float32
VMEM = pl.BlockSpec(memory_space=pltpu.VMEM)
SMEM = pl.BlockSpec(memory_space=pltpu.SMEM)
ANY = pl.BlockSpec(memory_space=pl.ANY)
VMEM_LIMIT = 56 * 1024 * 1024
SPLIT = 2
WIDE = 512
GATHER, SCATTER = 32, 33


def dot(a, b):
    return jnp.dot(a, b, preferred_element_type=F32)


def dot_nt(a, b):
    return lax.dot_general(a, b, (((1,), (1,)), ((), ())), preferred_element_type=F32)


def dot_tn(a, b):
    return lax.dot_general(a, b, (((0,), (0,)), ((), ())), preferred_element_type=F32)


def one_hot(row, count):
    places = lax.broadcasted_iota(jnp.int32, (count, row.shape[1]), 0)
    return jnp.where(places == row, 1.0, 0.0).astype(BF)


def one_hot_rows(column, count):
    places = lax.broadcasted_iota(jnp.int32, (column.shape[0], count), 1)
    return jnp.where(places == column, 1.0, 0.0).astype(BF)


def split3(x):
    high = x.astype(BF)
    rest = x - high.astype(F32)
    middle = rest.astype(BF)
    return high, middle, (rest - middle.astype(F32)).astype(BF)


def shape(dims, kind):
    return jax.ShapeDtypeStruct(dims, kind)


def call(kernel, outs, out_specs, ins, *args, scratch=(), flops=0):
    size = sum(a.size * a.dtype.itemsize for a in args) + sum(o.size * o.dtype.itemsize for o in outs)
    return pl.pallas_call(
        kernel,
        out_shape=tuple(outs),
        in_specs=ins,
        out_specs=tuple(out_specs),
        scratch_shapes=scratch,
        compiler_params=pltpu.CompilerParams(vmem_limit_bytes=VMEM_LIMIT),
        cost_estimate=pl.CostEstimate(flops=flops, bytes_accessed=size, transcendentals=0),
    )(*args)


def pack_kernel(counts_ref, rel_ref, src_ref, dst_ref, group_ref, out_ref, *, ents, n_ent):
    slots = rel_ref.shape[1]
    cap = slots // n_ent
    ent = lax.axis_index("ent")
    lane = lax.broadcasted_iota(jnp.int32, (1, slots), 1)
    block = lane // cap
    limit = jnp.zeros((1, slots), jnp.int32)
    last = jnp.zeros((1, slots), jnp.int32)
    for k in range(n_ent):
        limit = jnp.where(block == k, counts_ref[0, 0, k], limit)
        last = jnp.where(lane == k, counts_ref[0, 0, k], last)
    live = lane - block * cap < limit
    group = group_ref[...]
    digits = jnp.concatenate([group // 128, group % 128, jnp.zeros((14, group.shape[1]), jnp.int32)], axis=0)
    got = dot(digits.astype(F32).astype(BF), one_hot(rel_ref[...], group.shape[1])).astype(jnp.int32)
    packed = jnp.concatenate([
        got[0:1] * 128 + got[1:2],
        src_ref[...] - ent * ents,
        jnp.where(live, dst_ref[...] - block * ents, -1),
        last,
    ], axis=0)

    def put(i, carry):
        out_ref[i] = packed
        return carry

    lax.fori_loop(0, out_ref.shape[0], put, 0)


def table_kernel(pos_ref, coeffs_ref, pieces_ref, own_ref):
    basis_count = coeffs_ref.shape[0]
    n_high = coeffs_ref.shape[1] // 128
    values = coeffs_ref[...]
    mine = coeffs_ref[pl.ds(pos_ref[0], 1), :]
    n = n_high * basis_count
    for h in range(n_high):
        for i, piece in enumerate(split3(values[:, h * 128:(h + 1) * 128])):
            pieces_ref[i * n + h * basis_count:i * n + (h + 1) * basis_count, :] = piece
    own = [mine[:, h * 128:(h + 1) * 128] for h in range(n_high)]
    own.append(jnp.zeros((own_ref.shape[0] // 3 - n_high, 128), F32))
    own_ref[...] = jnp.concatenate(split3(jnp.concatenate(own, axis=0)), axis=0)


def coefficients(pieces, rel_row, basis_count, n_high):
    high = rel_row // 128
    got = dot(pieces, one_hot(rel_row % 128, 128))
    n = n_high * basis_count
    got = got[:n] + got[n:2 * n] + got[2 * n:]
    total = jnp.zeros((basis_count, rel_row.shape[1]), F32)
    for i in range(n_high):
        total += jnp.where(high == i, got[i * basis_count:(i + 1) * basis_count], 0.0)
    return total


def slot_rows(coef, gather, scatter):
    basis_count, lanes = coef.shape
    wide = -(-lanes // 128) * 128
    rows = jnp.concatenate(
        [coef, gather.astype(F32), scatter.astype(F32), jnp.zeros((128 - basis_count - 2, lanes), F32)], axis=0
    )
    if wide != lanes:
        rows = jnp.concatenate([rows, jnp.zeros((128, wide - lanes), F32)], axis=1)
    return rows.T[:lanes]


def clear_rows(ref):
    lane = lax.broadcasted_iota(jnp.int32, ref.shape, 1)
    ref[...] = jnp.where((lane == GATHER) | (lane == SCATTER), -1.0, 0.0)


def put_blocks(ref, rows, at, cap, counts):
    for g, count in enumerate(counts):
        ref[pl.ds(pl.multiple_of(at, 8), cap), :] = rows[g * cap:(g + 1) * cap]
        at = at + (count + 7) // 8 * 8
    return at


def prep_in_kernel(counts_ref, meta_ref, pieces_ref, rows_ref, ends_ref, *, n_rel, n_ent, ents, count):
    ent = lax.axis_index("ent")
    slots = meta_ref.shape[2]
    cap = slots // n_ent
    n_high = pieces_ref.shape[0] // (3 * count)
    clear_rows(rows_ref)

    def sender(m, at):
        s = ent ^ m
        ends_ref[m] = at
        block = jnp.concatenate(
            [pltpu.roll(meta_ref[g * n_ent + s], slots - ent * cap, 1)[:, :cap] for g in range(n_rel)], axis=1
        )
        coef = coefficients(pieces_ref[...], block[0:1, :], count, n_high)
        rows = slot_rows(coef, block[1:2, :] + m * ents, block[2:3, :])
        return put_blocks(rows_ref, rows, at, cap, [counts_ref[g * n_ent + s, ent] for g in range(n_rel)])

    ends_ref[n_ent] = lax.fori_loop(0, n_ent, sender, jnp.int32(0), unroll=n_ent <= 8)


def prep_rest_kernel(counts_ref, meta_ref, pieces_ref, own_ref, slots_ref, coef_b_ref, rows_ref, ends_ref,
                     *, n_rel, n_ent, ents, count):
    ent = lax.axis_index("ent")
    cap = meta_ref.shape[2] // n_ent
    lanes = n_rel * cap
    n_high = pieces_ref.shape[0] // (3 * count)
    n_own = own_ref.shape[0] // 3
    clear_rows(rows_ref)

    def regroup(s, carry):
        for g in range(n_rel):
            block = meta_ref[g * n_ent + s]
            for k in range(n_ent):
                slots_ref[s, k, :, g * cap:(g + 1) * cap] = block[:, k * cap:(k + 1) * cap]
        return carry

    lax.fori_loop(0, n_ent, regroup, 0, unroll=n_ent <= 8)

    def receiver(n, at):
        k = ent ^ n
        ends_ref[n] = at
        block = slots_ref[ent, k]
        coef = coefficients(pieces_ref[...], block[0:1, :], count, n_high)
        live = block[2:3, :] >= 0
        rows = slot_rows(coef, jnp.where(live, block[2:3, :] + n * ents, -1), jnp.where(live, block[1:2, :], -1))
        return put_blocks(rows_ref, rows, at, cap, [counts_ref[g * n_ent + ent, k] for g in range(n_rel)])

    ends_ref[n_ent] = lax.fori_loop(0, n_ent, receiver, jnp.int32(0), unroll=n_ent <= 8)

    def sender(s, carry):
        rel = jnp.concatenate([slots_ref[s, k, 0:1, :] for k in range(n_ent)], axis=1)
        got = dot(own_ref[...], one_hot(rel % 128, 128))
        got = got[:n_own] + got[n_own:2 * n_own] + got[2 * n_own:]
        mine = lax.broadcasted_iota(jnp.int32, got.shape, 0) == rel // 128
        picked = jnp.sum(jnp.where(mine, got, 0.0), axis=0, keepdims=True)
        for k in range(n_ent):
            coef_b_ref[s, k] = picked[:, k * lanes:(k + 1) * lanes]
        return carry

    lax.fori_loop(0, n_ent, sender, 0, unroll=n_ent <= 8)


def chunk_copies(refs, places, out_ref, sems):
    copies = []
    for i, (ref, place) in enumerate(zip(refs, places, strict=True)):
        if place is None:
            target = out_ref
        else:
            target = out_ref.at[place[0], pl.ds(place[1], ref.shape[0])]
        copies.append(pltpu.make_async_copy(ref, target, sems.at[i]))
    return copies


def gather_rows(rows_ref, ends_ref, pick, out_ref, lanes, ents, n_ent):
    last = jnp.minimum(ends_ref[n_ent] // WIDE, out_ref.shape[0] // WIDE - 1)
    out_ref[pl.ds(pl.multiple_of(last * WIDE, WIDE), WIDE), :] = jnp.zeros((WIDE, out_ref.shape[1]), F32)

    def chunk(m, carry):
        at = pl.multiple_of(ends_ref[m], 8)
        column = rows_ref[pl.ds(at, lanes), GATHER:GATHER + 1].astype(jnp.int32)
        pick(m, one_hot_rows(column - m * ents, ents), pl.ds(at, lanes))
        return carry

    lax.fori_loop(0, n_ent, chunk, 0, unroll=n_ent <= 8)


def apply_bases(picked, weight, rows_ref, start, size, count):
    total = None
    for b in range(count):
        part = weight(b, picked) * rows_ref[pl.ds(start, size), b:b + 1]
        total = part if total is None else total + part
    return total


WAIT_STEPS = (0, 4, 12)


def waited(weights, weight):
    def run(b, value):
        if b in WAIT_STEPS:
            later = [x for x in WAIT_STEPS if x > b] + [len(weights)]
            for c in weights[b:later[0]]:
                c.wait()
        return weight(b, value)

    return run


def for_tiles(end, narrow, tile, first):
    first(0, WIDE)
    wide = jnp.maximum(end // WIDE, 1)
    lax.fori_loop(1, wide, lambda t, c: (tile(pl.multiple_of(t * WIDE, WIDE), WIDE), c)[1], 0)
    done = wide * WIDE
    rest = (jnp.maximum(end - done, 0) + narrow - 1) // narrow
    lax.fori_loop(0, rest, lambda t, c: (tile(pl.multiple_of(done + t * narrow, narrow), narrow), c)[1], 0)


def forward_kernel(*refs, places, n_ent, count):
    n_parts = len(places)
    ends_ref, rows_ref, basis_ref, wself_ref, cot_ref = refs[:5]
    chunk_refs = refs[5:5 + n_parts]
    out_ref, grad_ref, scaled_ref = refs[5 + n_parts:8 + n_parts]
    feat_ref, weights_ref, x_ref, sums_ref, sems, weight_sems = refs[8 + n_parts:]
    cols = weights_ref.shape[2]
    ents = feat_ref.shape[1]
    half = lax.axis_index("rel") % SPLIT
    loads = chunk_copies(chunk_refs, places, feat_ref, sems)
    for c in loads:
        c.start()
    weights = [
        pltpu.make_async_copy(
            basis_ref.at[b, :, pl.ds(pl.multiple_of(half * cols, cols), cols)], weights_ref.at[b], weight_sems.at[b]
        )
        for b in range(count)
    ]
    sums_ref[...] = jnp.zeros_like(sums_ref)
    for c in loads:
        c.wait()
    for c in weights:
        c.start()

    def pick(m, hot, place):
        x_ref[place, :] = dot(hot, feat_ref[m])

    gather_rows(rows_ref, ends_ref, pick, x_ref, x_ref.shape[0] // n_ent, ents, n_ent)

    def weight(b, value):
        return dot(value, weights_ref[b])

    def tile(start, size, weight=weight):
        picked = x_ref[pl.ds(start, size), :].astype(BF)
        sent = apply_bases(picked, weight, rows_ref, start, size, count).astype(BF)
        hot = one_hot_rows(rows_ref[pl.ds(start, size), SCATTER:SCATTER + 1].astype(jnp.int32), ents)
        sums_ref[...] += dot_tn(hot, jnp.concatenate([sent, jnp.ones((size, 128), BF)], axis=1))

    for_tiles(ends_ref[n_ent], 128, tile, lambda start, size: tile(start, size, waited(weights, weight)))
    inverse = 1.0 / jnp.maximum(sums_ref[:, cols:cols + 1], 1.0)
    pre = dot(feat_ref[0], wself_ref[...]) + sums_ref[:, :cols] * inverse
    sig = jax.nn.sigmoid(pre)
    out_ref[...] = (pre * sig).astype(BF)
    grad = (cot_ref[...].astype(F32) * (sig * (1.0 + pre * (1.0 - sig)))).astype(BF)
    grad_ref[...] = grad
    scaled_ref[...] = (grad.astype(F32) * inverse).astype(BF)


def mix_chunks(first_row, slots_ref, coef_ref, feat_ref, mix_ref, hot_ref, out_ref, chunks):
    ent = lax.axis_index("ent")
    n_ent, ents = feat_ref.shape[:2]
    lanes = slots_ref.shape[3]
    rows = out_ref.shape[1]

    def receiver(i, carry):
        k = ent ^ (chunks[0] + i)
        for m in range(n_ent):
            s = ent ^ m
            at = slice(m * lanes, (m + 1) * lanes)
            got = dot_tn(feat_ref[m, :, pl.ds(first_row, rows)], one_hot(slots_ref[s, k, 1:2, :], ents))
            mix_ref[:, at] = (got * coef_ref[s, k]).astype(BF)
            hot_ref[:, at] = one_hot(slots_ref[s, k, 2:3, :], ents)
        out_ref[i] = dot_nt(mix_ref[...], hot_ref[...]).astype(BF)
        return carry

    lax.fori_loop(0, chunks[1] - chunks[0], receiver, 0)


def mix_kernel(*refs, places, chunks):
    n_parts = len(places)
    pos_ref, slots_ref, coef_ref = refs[:3]
    chunk_refs = refs[3:3 + n_parts]
    mix_out_ref = refs[3 + n_parts]
    feat_ref, mix_ref, hot_ref, sems = refs[4 + n_parts:]
    loads = chunk_copies(chunk_refs, places, feat_ref, sems)
    for c in loads:
        c.start()
    for c in loads:
        c.wait()
    mix_chunks(pl.multiple_of(pos_ref[1], 128), slots_ref, coef_ref, feat_ref, mix_ref, hot_ref, mix_out_ref, chunks)


def backward_kernel(*refs, places, n_ent, count):
    n_parts = len(places)
    ends_ref, rows_ref, basis_ref, wself_ref, pre_ref, other_ref = refs[:6]
    chunk_refs = refs[6:6 + 2 * n_parts]
    out_ref = refs[6 + 2 * n_parts]
    grad_ref, weights_ref, h_ref, sums_ref, sems, weight_sems = refs[7 + 2 * n_parts:]
    cols = weights_ref.shape[1]
    ents = grad_ref.shape[2]
    half = lax.axis_index("rel") % SPLIT
    own_at = pl.multiple_of(half * cols, cols)
    other_at = pl.multiple_of((1 - half) * cols, cols)
    loads = chunk_copies(chunk_refs[:n_parts], places, grad_ref.at[0], sems.at[0])
    loads += chunk_copies(chunk_refs[n_parts:], places, grad_ref.at[1], sems.at[1])
    for c in loads:
        c.start()
    weights = [
        pltpu.make_async_copy(basis_ref.at[b, pl.ds(own_at, cols)], weights_ref.at[b], weight_sems.at[b])
        for b in range(count)
    ]
    sums_ref[...] = jnp.zeros_like(sums_ref)
    for c in loads:
        c.wait()
    for c in weights:
        c.start()

    def pick(n, hot, place):
        h_ref[place, pl.ds(own_at, cols)] = dot(hot, grad_ref[0, n])
        h_ref[place, pl.ds(other_at, cols)] = dot(hot, grad_ref[1, n])

    gather_rows(rows_ref, ends_ref, pick, h_ref, h_ref.shape[0] // n_ent, ents, n_ent)

    def weight(b, value):
        return dot_nt(value, weights_ref[b])

    def tile(start, size, weight=weight):
        picked = h_ref[pl.ds(start, size), :].astype(BF)
        total = apply_bases(picked, weight, rows_ref, start, size, count)
        sent = total.astype(BF)
        hot = one_hot_rows(rows_ref[pl.ds(start, size), SCATTER:SCATTER + 1].astype(jnp.int32), ents)
        sums_ref[...] += dot_tn(hot, sent)

    for_tiles(ends_ref[n_ent], 256, tile, lambda start, size: tile(start, size, waited(weights, weight)))
    self_part = dot_nt(pre_ref[...], wself_ref[:, pl.ds(own_at, cols)])
    self_part += dot_nt(other_ref[...], wself_ref[:, pl.ds(other_at, cols)])
    out_ref[...] = (self_part + sums_ref[...]).astype(BF)


def basis_kernel(*refs, feat_places, places, chunks):
    n_feats, n_parts = len(feat_places), len(places)
    pos_ref, slots_ref, coef_ref, done_ref = refs[:4]
    feat_refs = refs[4:4 + n_feats]
    chunk_refs = refs[4 + n_feats:4 + n_feats + 2 * n_parts]
    out_ref = refs[4 + n_feats + 2 * n_parts]
    (feat_ref, mix_ref, hot_ref, grad_ref, early_ref, rest_ref, feat_sems, sems, early_sem) = (
        refs[5 + n_feats + 2 * n_parts:]
    )
    cols = grad_ref.shape[3]
    half = lax.axis_index("rel") % SPLIT
    feat_loads = chunk_copies(feat_refs, feat_places, feat_ref, feat_sems)
    loads = chunk_copies(chunk_refs[:n_parts], places, grad_ref.at[0], sems.at[0])
    loads += chunk_copies(chunk_refs[n_parts:], places, grad_ref.at[1], sems.at[1])
    loads.append(pltpu.make_async_copy(done_ref, early_ref, early_sem))
    for c in feat_loads:
        c.start()
    for c in feat_loads:
        c.wait()
    for c in loads:
        c.start()
    mix_chunks(pl.multiple_of(pos_ref[1], 128), slots_ref, coef_ref, feat_ref, mix_ref, hot_ref, rest_ref, chunks)
    for c in loads:
        c.wait()
    for side in range(SPLIT):
        total, n = None, 0
        for mix in (early_ref, rest_ref):
            for i in range(mix.shape[0]):
                part = dot(mix[i], grad_ref[side, n])
                total = part if total is None else total + part
                n += 1
        at = (half if side == 0 else 1 - half) * cols
        out_ref[:, pl.ds(pl.multiple_of(at, cols), cols)] = total


def exchange(x, mask, axis):
    count = lax.axis_size(axis)
    return lax.ppermute(x, axis, [(i, i ^ mask) for i in range(count)])


def stacked(x):
    n_ent = lax.axis_size("ent")
    whole = lax.all_gather(x, "ent", axis=0)
    return whole[lax.axis_index("ent") ^ jnp.arange(n_ent, dtype=jnp.int32)]


def feature_chunks(x, first, second):
    if lax.axis_size("ent") != 8:
        return [second(first([stacked(x)]))[0]], [None]
    rows = x.shape[0] // 2
    a, b = first([exchange(x, 2, "ent"), exchange(x, 4, "ent")])
    c = exchange(x, 1, "ent")
    top, low = second([exchange(b[:rows], 2, "ent"), exchange(a[rows:], 4, "ent")])
    parts = [x, c, a, exchange(a, 1, "ent"), b, exchange(b, 1, "ent")]
    parts += [top, low, exchange(top, 1, "ent"), exchange(low, 1, "ent")]
    return parts, [(m, 0) for m in range(6)] + [(6, 0), (6, rows), (7, 0), (7, rows)]


def half_chunks(own, other_of, first, second):
    if lax.axis_size("ent") != 8:
        (other,) = second(first([other_of()]))
        return [stacked(own)], [stacked(other)], [None]
    a0, b0, d0, c0 = [exchange(own, m, "ent") for m in (2, 4, 6, 1)]
    other, a0, b0, c0 = first([other_of(), a0, b0, c0])
    a1, b1, d1 = [exchange(other, m, "ent") for m in (2, 4, 6)]
    other, a0, b0, d0, a1, b1, d1 = second([other, a0, b0, d0, a1, b1, d1])
    c1, ca0, cb0, cd0, ca1, cb1, cd1 = [exchange(x, 1, "ent") for x in (other, a0, b0, d0, a1, b1, d1)]
    return [own, c0, a0, ca0, b0, cb0, d0, cd0], [other, c1, a1, ca1, b1, cb1, d1, cd1], [(m, 0) for m in range(8)]


def join_kernel(*refs):
    n = len(refs) // 3
    half = lax.axis_index("rel") % SPLIT
    for own, other, out in zip(refs[:n], refs[n:2 * n], refs[2 * n:], strict=True):
        cols = own.shape[1]
        out[:, pl.ds(pl.multiple_of(half * cols, cols), cols)] = own[...]
        out[:, pl.ds(pl.multiple_of((1 - half) * cols, cols), cols)] = other[...]


def per_device(features, w_self, basis_mats, basis_coeffs, group_rels, rel_local, edge_src,
               edge_dst, block_counts, cotangent):
    ents, depth = features.shape
    n_ent, n_rel = lax.axis_size("ent"), lax.axis_size("rel")
    slots = rel_local.shape[0]
    cap = slots // n_ent
    lanes = n_rel * cap
    n_rels, count = basis_coeffs.shape
    n_dev = n_rel * n_ent
    rows = count * depth // n_dev
    cols = depth // SPLIT
    rel = lax.axis_index("rel")
    half = rel % SPLIT
    all_lanes = n_ent * lanes

    (meta,) = call(
        functools.partial(pack_kernel, ents=ents, n_ent=n_ent),
        [shape((n_dev, 4, slots), jnp.int32)], [VMEM], [SMEM] + [VMEM] * 4,
        block_counts, rel_local[None], edge_src[None], edge_dst[None],
        group_rels[None],
    )
    meta = lax.all_to_all(meta, ("rel", "ent"), 0, 0, tiled=True)
    counts = meta[:, 3, :n_ent]

    first_row = (rel * n_ent + lax.axis_index("ent")) * rows
    pos = jnp.stack([first_row // depth, first_row % depth]).astype(jnp.int32)
    basis = basis_mats.reshape(count, depth, depth)
    wself_cols = lax.dynamic_slice_in_dim(w_self, half * cols, cols, axis=1)
    wself_rows = lax.dynamic_slice_in_dim(w_self, half * cols, cols, axis=0)
    cot = lax.dynamic_slice_in_dim(cotangent, half * cols, cols, axis=1)
    padded = -(-n_rels // 128) * 128
    coeffs_t = jnp.pad(basis_coeffs, ((0, padded - n_rels), (0, 0))).T

    n_high = padded // 128
    n_own = -(-(n_high + 1) // 16) * 16
    pieces, own_pieces = call(
        table_kernel,
        [shape((3 * n_high * count, 128), BF), shape((3 * n_own, 128), BF)],
        [VMEM, VMEM], [SMEM, VMEM], pos, coeffs_t,
    )
    row_shape = shape((all_lanes, 128), F32)
    ends_shape = shape((n_ent + 1,), jnp.int32)
    inputs = [pieces, own_pieces, wself_cols, cot, wself_rows]

    def beside_first(arrived):
        tied = lax.optimization_barrier((*arrived, *inputs))
        inputs[:] = tied[len(arrived):]
        return tied[:len(arrived)]

    def beside_second(arrived):
        pieces = inputs[0]
        made = call(
            functools.partial(prep_in_kernel, n_rel=n_rel, n_ent=n_ent, ents=ents, count=count),
            [row_shape, ends_shape], [VMEM, SMEM], [SMEM, VMEM, VMEM],
            counts, meta, pieces,
            flops=10**9,
        )
        tied = lax.optimization_barrier((*arrived, *made))
        inputs.extend(tied[len(arrived):])
        return tied[:len(arrived)]

    feats, feat_places = feature_chunks(features, beside_first, beside_second)
    pieces, own_pieces, wself_cols, cot, wself_rows, rows_in, ends_in = inputs
    part_sems = pltpu.SemaphoreType.DMA((len(feats),))
    out_cols, pre_cols, scaled_cols = call(
        functools.partial(forward_kernel, places=feat_places, n_ent=n_ent, count=count),
        [shape((ents, cols), BF)] * 3, [VMEM] * 3,
        [SMEM, VMEM, ANY, VMEM, VMEM] + [ANY] * len(feats),
        ends_in, rows_in, basis, wself_cols, cot, *feats,
        scratch=[
            pltpu.VMEM((n_ent, ents, depth), BF),
            pltpu.VMEM((count, depth, cols), BF),
            pltpu.VMEM((all_lanes, depth), F32),
            pltpu.VMEM((ents, cols + 128), F32),
            part_sems,
            pltpu.SemaphoreType.DMA((count,)),
        ],
        flops=2 * all_lanes * count * depth * cols,
    )
    other_pre = []
    made = []

    def tie(arrived, *others):
        tied = lax.optimization_barrier((*arrived, *others))
        made.extend(tied[len(arrived):])
        return tied[:len(arrived)]

    def prep_rest(arrived):
        return tie(arrived, *call(
            functools.partial(prep_rest_kernel, n_rel=n_rel, n_ent=n_ent, ents=ents, count=count),
            [shape((n_ent, n_ent, 4, lanes), jnp.int32), shape((n_ent, n_ent, 1, lanes), F32), row_shape, ends_shape],
            [VMEM, VMEM, VMEM, SMEM], [SMEM, VMEM, VMEM, VMEM],
            counts, meta, pieces, own_pieces,
            flops=10**9,
        ))

    early = n_ent * 5 // 8
    mix_scratch = [
        pltpu.VMEM((n_ent, ents, depth), BF),
        pltpu.VMEM((rows, all_lanes), BF),
        pltpu.VMEM((ents, all_lanes), BF),
    ]

    def mix_early(arrived):
        other_pre.append(exchange(pre_cols, 1, "rel"))
        grouped, coef_b = made[:2]
        return tie(arrived, *call(
            functools.partial(mix_kernel, places=feat_places, chunks=(0, early)),
            [shape((early, rows, ents), BF)], [VMEM],
            [SMEM, VMEM, VMEM] + [ANY] * len(feats),
            pos, grouped, coef_b, *feats,
            scratch=mix_scratch + [part_sems],
            flops=10**9,
        ))

    own_parts, other_parts, places = half_chunks(
        scaled_cols, lambda: exchange(scaled_cols, 1, "rel"), prep_rest, mix_early
    )
    grouped, coef_b, rows_out, ends_out, mixed = made
    (other_pre,) = other_pre

    grad_scratch = pltpu.VMEM((SPLIT, n_ent, ents, cols), BF)
    grad_sems = pltpu.SemaphoreType.DMA((SPLIT, len(own_parts)))
    (grad_cols,) = call(
        functools.partial(backward_kernel, places=places, n_ent=n_ent, count=count),
        [shape((ents, cols), BF)], [VMEM],
        [SMEM, VMEM, ANY, VMEM, VMEM, VMEM] + [ANY] * (2 * len(own_parts)),
        ends_out, rows_out, basis, wself_rows, pre_cols, other_pre, *own_parts, *other_parts,
        scratch=[
            grad_scratch,
            pltpu.VMEM((count, cols, depth), BF),
            pltpu.VMEM((all_lanes, depth), F32),
            pltpu.VMEM((ents, cols), F32),
            grad_sems,
            pltpu.SemaphoreType.DMA((count,)),
        ],
        flops=2 * all_lanes * count * depth * cols,
    )
    grad_cols, out_cols, pos = lax.optimization_barrier((grad_cols, out_cols, pos))
    other_grad, other_out = exchange(grad_cols, 1, "rel"), exchange(out_cols, 1, "rel")
    (grad_basis,) = call(
        functools.partial(basis_kernel, feat_places=feat_places, places=places, chunks=(early, n_ent)),
        [shape((rows, depth), F32)], [VMEM],
        [SMEM, VMEM, VMEM] + [ANY] * (1 + len(feats) + 2 * len(own_parts)),
        pos, grouped, coef_b, mixed, *feats, *own_parts, *other_parts,
        scratch=mix_scratch + [
            grad_scratch,
            pltpu.VMEM((early, rows, ents), BF),
            pltpu.VMEM((n_ent - early, rows, ents), BF),
            part_sems,
            grad_sems,
            pltpu.SemaphoreType.DMA,
        ],
        flops=2 * n_ent * rows * ents * depth,
    )
    activations, grad_features = call(
        join_kernel, [shape((ents, depth), BF)] * 2, [VMEM] * 2, [VMEM] * 4, out_cols, grad_cols, other_out, other_grad
    )
    return activations, grad_features, grad_basis


def solution(mesh):
    placed = (
        P("ent", None),
        P(),
        P(),
        P(),
        P("rel"),
        P(("rel", "ent")),
        P(("rel", "ent")),
        P(("rel", "ent")),
        P("rel", "ent", None),
        P("ent", None),
    )
    return jax.shard_map(
        per_device,
        mesh=mesh,
        in_specs=placed,
        out_specs=(P("ent", None), P("ent", None), P(("rel", "ent"), None)),
        check_vma=False,
    )
```
